256 devices in a mesh: grp: 16 (over z_hi, y), row: 16 (over z_lo, x, core).
Axes of the slice: x: 4, y: 4, z: 8 (z_hi: 4, z_lo: 2; z = z_hi * 2 + z_lo), core: 2. Of those that a mesh axis runs over, the one named last changes fastest.
Arguments:
- grads: float32 [24, 16, 448, 1024], P(None, 'row', 'grp'), may hold values from -320 to 320
- momentum: float32 [24, 16, 448, 1024], P(None, 'row', 'grp'), may hold values from -640 to 640
- owner_table: int32 [24], replicated, may hold values from 0 to 16, as said below
Outputs:
- new_momentum: float32 [24, 16, 448, 1024], P(None, 'row', 'grp')
- update: float32 [24, 16, 448, 1024], P(None, 'row', 'grp')
The draws below stay inside these ranges and needn't reach their ends.
Inputs may be any that keep to these rules, and one draw needn't show every extreme that they name: `owner_table`: each value 0 to 15 appears exactly once; the other entries equal 16.
All inputs are finite; a program needn't handle non-finite values.
Results may differ from the reference program's by a relative error of at most 0.0001.
Values sent between devices are 32-bit elements; how exact they have to be, the bound alone decides.
No kernel may reach another device: no remote copies, remote signals or barrier semaphores. Data moves between devices by JAX's collectives and lax.ppermute only.
A program may use at most 64 MiB of HBM per device.

```python
import math
import jax
import jax.numpy as jnp
from jax import lax

ROWS = 7168
C = 1024
ITERS = 2
GROUPS = 16
BLOCKS = 16
MATS = 24
BLOCK_ROWS = 448


def shared_scales(key, spread):
    key_rows, key_cols = jax.random.split(key)
    row_scale = jnp.exp(jax.random.uniform(key_rows, (MATS, ROWS), jnp.float32, 0.0, math.log(spread)))
    col_scale = jnp.exp(jax.random.uniform(key_cols, (MATS, C), jnp.float32, 0.0, math.log(spread)))
    return (row_scale, col_scale)


def assemble(noise, row_scale, col_scale, rise, factor):
    grade = jnp.arange(ROWS, dtype=jnp.float32) / (ROWS - 1)
    lift = rise ** (0.5 * grade)
    rows_total = (row_scale * lift[None, :]).reshape(MATS, BLOCKS, BLOCK_ROWS, 1)
    return jnp.clip(noise, -4.0, 4.0) * rows_total * col_scale[:, None, None, :] * factor


def draw_grads(key, part):
    row_scale, col_scale = shared_scales(key, 10.0)
    key = jax.random.fold_in(key, 11)
    shape = (MATS, BLOCKS, BLOCK_ROWS, C)
    noise = jax.random.normal(key, shape, jnp.float32)
    return assemble(noise, row_scale, col_scale, 3.0, 0.1)


def draw_momentum(key, part):
    row_scale, col_scale = shared_scales(key, 10.0)
    key = jax.random.fold_in(key, 12)
    shape = (MATS, BLOCKS, BLOCK_ROWS, C)
    noise = jax.random.normal(key, shape, jnp.float32)
    return assemble(noise, row_scale, col_scale, 3.0, 0.2)


def draw_owner_table(key, part):
    key = jax.random.fold_in(key, 13)
    order = jax.random.permutation(key, MATS).astype(jnp.int32)
    return jnp.minimum(order, GROUPS).astype(jnp.int32)


def setup_inputs(seed: int = 0) -> dict:
    splits = jax.random.split(jax.random.key(seed), 4)
    grads = draw_grads(jax.random.fold_in(splits[3], 71), 0)
    momentum = draw_momentum(jax.random.fold_in(splits[3], 71), 0)
    owner_table = draw_owner_table(jax.random.fold_in(splits[3], 71), 0)
    return {"grads": grads, "momentum": momentum, "owner_table": owner_table}


momentum_decay = 0.95
norm_epsilon = 1e-07
first_coef = 3.4445
second_coef = -4.775
third_coef = 2.0315

def high_dot(left, right):
    return jnp.dot(left, right, precision=lax.Precision.HIGHEST, preferred_element_type=jnp.float32)

def newton(matrix):
    total = jnp.sum(matrix * matrix)
    current = matrix / (jnp.sqrt(total) + norm_epsilon)
    for step in range(ITERS):
        gram = high_dot(current.T, current)
        product = high_dot(current, gram)
        current = first_coef * current + second_coef * product + third_coef * high_dot(product, gram)
    return current * (0.2 * math.sqrt(max(ROWS, C)))

def reference(grads, momentum, owner_table):
    in_window = owner_table < GROUPS
    flags = in_window[:, None, None, None]
    new_momentum = jnp.where(flags, momentum_decay * momentum + grads, momentum)
    nesterov = grads + momentum_decay * new_momentum
    group_ids = jnp.arange(GROUPS, dtype=jnp.int32)
    matches = (owner_table[None, :] == group_ids[:, None]).astype(jnp.int32)
    chosen = lax.optimization_barrier(jnp.sum(matches * jnp.arange(MATS, dtype=jnp.int32)[None, :], axis=1)).astype(jnp.int32)
    selected = jnp.take(nesterov, chosen, axis=0)

    def one_matrix(stack):
        return newton(stack.reshape(ROWS, C)).reshape(BLOCKS, BLOCK_ROWS, C)
    results = lax.map(one_matrix, selected)
    picked = jnp.take(results, jnp.minimum(owner_table, GROUPS - 1).astype(jnp.int32), axis=0)
    update = jnp.where(flags, picked, jnp.zeros_like(picked))
    return (new_momentum, update)
```

```python
import math

import jax
import jax.numpy as jnp
from jax import lax
from jax.experimental import pallas as pl
from jax.experimental.pallas import tpu as pltpu
from jax.sharding import PartitionSpec as P

MATS = 24
GROUPS = 16
PIECE = 28
MSG = 4 * PIECE
C = 1024
ROWS = 7168
TILE = 256
NT = C // TILE
BLK = 128
NB = C // BLK
TRI = NB * (NB + 1) // 2
PART = TRI * BLK // 8
HALF = PART // 2
SHARE = 4 * PART

momentum_decay = 0.95
norm_epsilon = 1e-07
first_coef = 3.4445
second_coef = -4.775
third_coef = 2.0315
out_scale = 0.2 * math.sqrt(max(ROWS, C))

f32 = jnp.float32
bf16 = jnp.bfloat16
ALL = ("grp", "row")


def coords(n):
    core = n % 2
    x = (n // 2) % 4
    z_lo = (n // 8) % 2
    y = (n // 16) % 4
    z_hi = n // 64
    return (x, y, z_hi * 2 + z_lo, core)


def number(x, y, z, core):
    return ((((z // 2) * 4 + y) * 2 + z % 2) * 4 + x) * 2 + core


def pairs(move):
    out = []
    for n in range(256):
        x, y, z, core = coords(n)
        out.append((n, number(*move(x, y, z, core))))
    return out


def first_axis(step):
    return pairs(
        lambda x, y, z, c: ((x + step) % 4, y, z, c) if c == 0 else (x, (y + step) % 4, z, c)
    )


def second_axis(step):
    return pairs(
        lambda x, y, z, c: (x, (y + step) % 4, z, c) if c == 0 else ((x + step) % 4, y, z, c)
    )


def permute(value, perm):
    return lax.ppermute(value, ALL, perm)


def swap_cores(value):
    return permute(value, pairs(lambda x, y, z, c: (x, y, z, 1 - c)))


def along_z(value):
    return permute(value, pairs(lambda x, y, z, c: (x, y, (z + 1 - 2 * c) % 8, c)))


def fill_chosen(table_ref, place_ref, chosen_ref):
    x, y, core = place_ref[0], place_ref[1], place_ref[3]
    for k in range(MATS):
        owner = table_ref[k]

        @pl.when(owner < GROUPS)
        def _():
            dx = ((owner & 3) - x) & 3
            dy = ((owner >> 2) - y) & 3
            slot = jnp.where(core == 0, dx * 4 + dy, dy * 4 + dx)
            chosen_ref[slot] = k


def outgoing_kernel(table_ref, place_ref, grads_ref, mom_ref, o0, o1, o2, o3, chosen_ref, gbuf, mbuf, sems):
    fill_chosen(table_ref, place_ref, chosen_ref)

    def copies(slot):
        k = chosen_ref[slot]
        return (
            pltpu.make_async_copy(grads_ref.at[k, 0], gbuf.at[slot], sems.at[0, slot]),
            pltpu.make_async_copy(mom_ref.at[k, 0], mbuf.at[slot], sems.at[1, slot]),
        )

    for slot in range(GROUPS):
        for copy in copies(slot):
            copy.start()
    outs = (o0, o1, o2, o3)
    for slot in range(GROUPS):
        for copy in copies(slot):
            copy.wait()
        g = gbuf[slot]
        new = momentum_decay * mbuf[slot] + g
        t = slot % 4
        outs[slot // 4][t * PIECE : (t + 1) * PIECE, :] = g + momentum_decay * new


def regroup_kernel(i0, i1, i2, i3, o0, o1, o2, o3):
    ins, outs = (i0, i1, i2, i3), (o0, o1, o2, o3)
    for t in range(4):
        for s in range(4):
            outs[t][s * PIECE : (s + 1) * PIECE, :] = ins[s][t * PIECE : (t + 1) * PIECE, :]


def split(value):
    hi = value.astype(bf16)
    return hi, (value - hi.astype(f32)).astype(bf16)


def dot(left, right):
    return jnp.dot(left, right, preferred_element_type=f32)


def block_index(i, j):
    return i * NB - i * (i - 1) // 2 + (j - i)


def rows(start, size):
    return pl.ds(pl.multiple_of(start, 8), size)


def gram_kernel(place_ref, q0, q1, q2, q3, keep_ref, give_ref, hi_ref, lo_ref, hit_ref, lot_ref, gram_ref):
    for t, q in enumerate((q0, q1, q2, q3)):
        hi, lo = split(q[...])
        at = slice(t * MSG, (t + 1) * MSG)
        hi_ref[at, :] = hi
        lo_ref[at, :] = lo
    hit_ref[...] = hi_ref[...].T
    lot_ref[...] = lo_ref[...].T
    for p in range(NT):
        r = slice(p * TILE, (p + 1) * TILE)
        w = slice(p * TILE, C)
        acc = dot(hit_ref[r, :], hi_ref[:, w])
        acc = acc + dot(hit_ref[r, :], lo_ref[:, w])
        acc = acc + dot(lot_ref[r, :], hi_ref[:, w])
        for i in (2 * p, 2 * p + 1):
            for j in range(i, NB):
                b = block_index(i, j)
                gram_ref[b * BLK : (b + 1) * BLK, :] = acc[
                    (i - 2 * p) * BLK : (i - 2 * p + 1) * BLK, (j - 2 * p) * BLK : (j - 2 * p + 1) * BLK
                ]
    z, core = place_ref[2], place_ref[3]
    for out_ref, c in ((keep_ref, core), (give_ref, 1 - core)):
        way = 1 - 2 * c
        for i in (1, 2, 3):
            d = (z + way * i) & 7
            base = (i - 1) * PART
            out_ref[base : base + HALF, :] = gram_ref[rows(d * PART + c * HALF, HALF), :]
            out_ref[base + HALF : base + PART, :] = gram_ref[rows(d * PART + (1 - c) * HALF, HALF), :]
        d = (z + 4) & 7
        out_ref[3 * PART : 3 * PART + HALF, :] = gram_ref[rows(d * PART + c * HALF, HALF), :]
        out_ref[3 * PART + HALF : SHARE, :] = gram_ref[rows(z * PART + c * HALF, HALF), :]


def diagonal(p, width):
    row = lax.broadcasted_iota(jnp.int32, (TILE, width), 0)
    col = lax.broadcasted_iota(jnp.int32, (TILE, width), 1)
    return row == col


def put(p, value, h_ref, l_ref):
    hi, lo = split(value)
    r = slice(p * TILE, (p + 1) * TILE)
    h_ref[r, p * TILE :] = hi
    l_ref[r, p * TILE :] = lo
    for q in range(p + 1, NT):
        w = slice((q - p) * TILE, (q - p + 1) * TILE)
        h_ref[q * TILE : (q + 1) * TILE, r] = hi[:, w].T
        l_ref[q * TILE : (q + 1) * TILE, r] = lo[:, w].T


def product_row(r, w, left, right):
    acc = dot(left[0][r, :], right[0][:, w])
    acc = acc + dot(left[0][r, :], right[1][:, w])
    return acc + dot(left[1][r, :], right[0][:, w])


def polynomial(s, out):
    for p in range(NT):
        r = slice(p * TILE, (p + 1) * TILE)
        w = slice(p * TILE, C)
        acc = third_coef * product_row(r, w, s, s)
        acc = acc + second_coef * (s[0][r, w].astype(f32) + s[1][r, w].astype(f32))
        acc = acc + jnp.where(diagonal(p, C - p * TILE), first_coef, 0.0)
        put(p, acc, out[0], out[1])


def symmetric_product(left, right, out):
    for p in range(NT):
        r = slice(p * TILE, (p + 1) * TILE)
        put(p, product_row(r, slice(p * TILE, C), left, right), out[0], out[1])


def step_kernel(
    place_ref, own, g1, g2, g3, g4, n1, n2, n3, n4, q0, q1, q2, q3, o0, o1, o2, o3,
    gram_ref, ah, al, bh, bl, ch, cl, xh, xl, yh, yl,
):
    z, core = place_ref[2], place_ref[3]
    far = (z + 4) & 7
    gram_ref[rows(z * PART + core * HALF, HALF), :] = own[:HALF, :]
    gram_ref[rows(z * PART + (1 - core) * HALF, HALF), :] = own[HALF:, :]
    gram_ref[rows(far * PART + core * HALF, HALF), :] = g4[...]
    gram_ref[rows(far * PART + (1 - core) * HALF, HALF), :] = n4[...]
    for c, parts in ((core, (g1, g2, g3)), (1 - core, (n1, n2, n3))):
        way = 1 - 2 * c
        for i, part in enumerate(parts):
            d = (z - way * (i + 1)) & 7
            gram_ref[rows(d * PART + c * HALF, HALF), :] = part[:HALF, :]
            gram_ref[rows(d * PART + (1 - c) * HALF, HALF), :] = part[HALF:, :]
    row = lax.broadcasted_iota(jnp.int32, (BLK, BLK), 0)
    col = lax.broadcasted_iota(jnp.int32, (BLK, BLK), 1)
    diag = jnp.zeros((BLK, BLK), f32)
    for i in range(NB):
        b = block_index(i, i)
        diag = diag + gram_ref[b * BLK : (b + 1) * BLK, :]
    diag = jnp.where(row == col, diag, 0.0)
    total = jnp.sum(jnp.sum(diag, axis=0, keepdims=True), axis=1, keepdims=True)
    inverse = 1.0 / (jnp.sqrt(total) + norm_epsilon)
    for i in range(NB):
        for j in range(i, NB):
            b = block_index(i, j)
            hi, lo = split(gram_ref[b * BLK : (b + 1) * BLK, :] * inverse * inverse)
            ri = slice(i * BLK, (i + 1) * BLK)
            rj = slice(j * BLK, (j + 1) * BLK)
            ah[ri, rj] = hi
            al[ri, rj] = lo
            if j > i:
                ah[rj, ri] = hi.T
                al[rj, ri] = lo.T
    for t, q in enumerate((q0, q1, q2, q3)):
        hi, lo = split(q[...])
        at = slice(t * MSG, (t + 1) * MSG)
        xh[at, :] = hi
        xl[at, :] = lo
    polynomial((ah, al), (bh, bl))
    for t in range(4):
        at = slice(t * MSG, (t + 1) * MSG)
        hi, lo = split(product_row(at, slice(0, C), (xh, xl), (bh, bl)))
        yh[at, :] = hi
        yl[at, :] = lo
    symmetric_product((ah, al), (bh, bl), (ch, cl))
    symmetric_product((ch, cl), (bh, bl), (ah, al))
    polynomial((ah, al), (bh, bl))
    factor = inverse * out_scale
    for t, out_ref in enumerate((o0, o1, o2, o3)):
        at = slice(t * MSG, (t + 1) * MSG)
        out_ref[...] = product_row(at, slice(0, C), (yh, yl), (bh, bl)) * factor


def update_kernel(table_ref, place_ref, i0, i1, i2, i3, update_ref, chosen_ref):
    fill_chosen(table_ref, place_ref, chosen_ref)
    for k in range(MATS):

        @pl.when(table_ref[k] >= GROUPS)
        def _():
            update_ref[k, 0] = jnp.zeros((PIECE, C), f32)

    ins = (i0, i1, i2, i3)
    for slot in range(GROUPS):
        t = slot % 4
        update_ref[chosen_ref[slot], 0] = ins[slot // 4][t * PIECE : (t + 1) * PIECE, :]


VMEM = pl.BlockSpec(memory_space=pltpu.VMEM)
SMEM = pl.BlockSpec(memory_space=pltpu.SMEM)
HBM = pl.BlockSpec(memory_space=pl.ANY)


def shape(*dims):
    return jax.ShapeDtypeStruct(dims, f32)


def call(kernel, in_specs, out_shape, scratch, name, flops, moved):
    return pl.pallas_call(
        kernel,
        in_specs=in_specs,
        out_specs=jax.tree.map(lambda _: VMEM, out_shape),
        out_shape=out_shape,
        scratch_shapes=scratch,
        name=name,
        cost_estimate=pl.CostEstimate(flops=flops, bytes_accessed=moved, transcendentals=0),
        compiler_params=pltpu.CompilerParams(vmem_limit_bytes=56 * 1024 * 1024),
    )


MESSAGES = [shape(MSG, C)] * 4
MSG_BYTES = 4 * MSG * C * 4


def shards(grads, momentum, owner_table):
    grp, row = lax.axis_index("grp"), lax.axis_index("row")
    core = row % 2
    place = jnp.stack([(row // 2) % 4, grp % 4, (grp // 4) * 2 + row // 8, core]).astype(jnp.int32)

    outgoing = call(
        outgoing_kernel, [SMEM, SMEM, HBM, HBM], MESSAGES,
        [
            pltpu.SMEM((GROUPS,), jnp.int32),
            pltpu.VMEM((GROUPS, PIECE, C), f32),
            pltpu.VMEM((GROUPS, PIECE, C), f32),
            pltpu.SemaphoreType.DMA((2, GROUPS)),
        ],
        "outgoing", 0, 3 * MSG_BYTES,
    )(owner_table, place, grads, momentum)

    regroup = call(regroup_kernel, [VMEM] * 4, MESSAGES, [], "regroup", 0, 2 * MSG_BYTES)
    arrived = [outgoing[0]] + [permute(outgoing[s], first_axis(s)) for s in (1, 2, 3)]
    forward = regroup(*arrived)
    owned = [forward[0]] + [permute(forward[t], second_axis(t)) for t in (1, 2, 3)]

    flags = (owner_table < GROUPS)[:, None, None, None]
    new_momentum = jnp.where(flags, momentum_decay * momentum + grads, momentum)

    keep, give = call(
        gram_kernel, [SMEM] + [VMEM] * 4, [shape(SHARE, BLK)] * 2,
        [
            pltpu.VMEM((4 * MSG, C), bf16),
            pltpu.VMEM((4 * MSG, C), bf16),
            pltpu.VMEM((C, 4 * MSG), bf16),
            pltpu.VMEM((C, 4 * MSG), bf16),
            pltpu.VMEM((TRI * BLK, BLK), f32),
        ],
        "gram", 6 * 4 * MSG * C * C // 2, MSG_BYTES + 8 * SHARE * BLK,
    )(place, *owned)

    chip = keep + swap_cores(give)
    near, middle, distant = chip[:PART], chip[PART : 2 * PART], chip[2 * PART : 3 * PART]
    farthest, mine = chip[3 * PART : 3 * PART + HALF], chip[3 * PART + HALF :]
    moving = along_z(farthest)
    moving = along_z(jnp.concatenate([distant[:HALF] + moving, distant[HALF:]]))
    moving = along_z(middle + moving)
    moving = along_z(near + moving)
    moving = jnp.concatenate([moving[:HALF] + mine, moving[HALF:]])
    other = swap_cores(moving)
    own = jnp.concatenate([moving[:HALF] + other[HALF:], moving[HALF:] + other[:HALF]])

    g1 = along_z(own)
    g2 = along_z(g1)
    g3 = along_z(g2)
    g4 = along_z(g3[:HALF])
    n1, n2, n3, n4 = swap_cores(g1), swap_cores(g2), swap_cores(g3), swap_cores(g4)

    square = [pltpu.VMEM((C, C), bf16)] * 6
    tall = [pltpu.VMEM((4 * MSG, C), bf16)] * 4
    results = call(
        step_kernel, [SMEM] + [VMEM] * 13, MESSAGES,
        [pltpu.VMEM((TRI * BLK, BLK), f32)] + square + tall,
        "newton", 6 * (4 * C * C * C * 5 // 8 + 2 * 4 * MSG * C * C), 2 * MSG_BYTES + 4 * TRI * BLK * BLK,
    )(place, own, g1, g2, g3, g4, n1, n2, n3, n4, *owned)

    back = [results[0]] + [permute(results[t], second_axis(-t)) for t in (1, 2, 3)]
    back = regroup(*back)
    back = [back[0]] + [permute(back[s], first_axis(-s)) for s in (1, 2, 3)]
    update = call(
        update_kernel, [SMEM, SMEM] + [VMEM] * 4, shape(MATS, 1, PIECE, C),
        [pltpu.SMEM((GROUPS,), jnp.int32)], "update", 0, 3 * MSG_BYTES,
    )(owner_table, place, *back)
    return (new_momentum, update)


def solution(mesh):
    in_specs = (P(None, "row", "grp", None), P(None, "row", "grp", None), P())
    out_specs = (P(None, "row", "grp", None), P(None, "row", "grp", None))
    return jax.shard_map(shards, mesh=mesh, in_specs=in_specs, out_specs=out_specs, check_vma=False)
```

```python
import math

import jax
import jax.numpy as jnp
from jax import lax
from jax.experimental import pallas as pl
from jax.experimental.pallas import tpu as pltpu
from jax.sharding import PartitionSpec as P

MATS = 24
GROUPS = 16
C = 1024
PIECE_ROWS = 14
LINES = PIECE_ROWS * C // 128
MSG_ROWS = 4 * PIECE_ROWS
MSG_LINES = 4 * LINES
BAND = 2 * MSG_ROWS
MOM_STEP = 4
ROWS = 7168
TILE = 256
NT = C // TILE
BLK = 128
NB = C // BLK
TRI = NB * (NB + 1) // 2
PART = TRI * BLK // 8
HALF = PART // 2

momentum_decay = 0.95
norm_epsilon = 1e-07
first_coef = 3.4445
second_coef = -4.775
third_coef = 2.0315
out_scale = 0.2 * math.sqrt(max(ROWS, C))

f32 = jnp.float32
bf16 = jnp.bfloat16
ALL = ("grp", "row")


def coords(n):
    core = n % 2
    x = (n // 2) % 4
    z_lo = (n // 8) % 2
    y = (n // 16) % 4
    z_hi = n // 64
    return (x, y, z_hi * 2 + z_lo, core)


def number(x, y, z, core):
    return ((((z // 2) * 4 + y) * 2 + z % 2) * 4 + x) * 2 + core


def pairs(move):
    out = []
    for n in range(256):
        x, y, z, core = coords(n)
        out.append((n, number(*move(x, y, z, core))))
    return out


def first_axis(step):
    return pairs(
        lambda x, y, z, c: ((x + step) % 4, y, z, c) if c == 0 else (x, (y + step) % 4, z, c)
    )


def second_axis(step):
    return pairs(
        lambda x, y, z, c: (x, (y + step) % 4, z, c) if c == 0 else ((x + step) % 4, y, z, c)
    )


def permute(value, perm):
    return lax.ppermute(value, ALL, perm)


def swap_cores(value):
    return permute(value, pairs(lambda x, y, z, c: (x, y, z, 1 - c)))


def along_z(value, step):
    return permute(value, pairs(lambda x, y, z, c: (x, y, (z + step * (1 - 2 * c)) % 8, c)))


def fill_chosen(table_ref, place_ref, chosen_ref):
    x, y, core = place_ref[0], place_ref[1], place_ref[3]
    for k in range(MATS):
        owner = table_ref[k]

        @pl.when(owner < GROUPS)
        def _():
            dx = ((owner & 3) - x) & 3
            dy = ((owner >> 2) - y) & 3
            slot = jnp.where(core == 0, dx * 4 + dy, dy * 4 + dx)
            chosen_ref[slot] = k


def outgoing_kernel(table_ref, place_ref, grads_ref, mom_ref, *refs):
    outs, (chosen_ref, gbuf, mbuf, sems) = refs[:8], refs[8:]
    fill_chosen(table_ref, place_ref, chosen_ref)

    def copies(slot):
        k = chosen_ref[slot]
        return (
            pltpu.make_async_copy(grads_ref.at[k], gbuf.at[slot], sems.at[0, slot]),
            pltpu.make_async_copy(mom_ref.at[k], mbuf.at[slot], sems.at[1, slot]),
        )

    for slot in range(GROUPS):
        for copy in copies(slot):
            copy.start()
    for slot in range(GROUPS):
        for copy in copies(slot):
            copy.wait()
        g = gbuf[slot]
        new = momentum_decay * mbuf[slot] + g
        nesterov = g + momentum_decay * new
        s, t = slot // 4, slot % 4
        for h in range(2):
            outs[4 * h + s][t * LINES : (t + 1) * LINES, :] = nesterov[h * LINES : (h + 1) * LINES, :]


def momentum_kernel(table_ref, grads_ref, mom_ref, new_ref):
    for i in range(MOM_STEP):
        k = pl.program_id(0) * MOM_STEP + i
        m = mom_ref[i]
        new_ref[i] = jnp.where(table_ref[k] < GROUPS, momentum_decay * m + grads_ref[i], m)


def regroup_kernel(i0, i1, i2, i3, o0, o1, o2, o3):
    ins, outs = (i0, i1, i2, i3), (o0, o1, o2, o3)
    for t in range(4):
        for s in range(4):
            outs[t][s * LINES : (s + 1) * LINES, :] = ins[s][t * LINES : (t + 1) * LINES, :]


def gather_rows(messages, x_ref):
    for h in range(2):
        for t in range(4):
            at = slice((h * 4 + t) * MSG_ROWS, (h * 4 + t + 1) * MSG_ROWS)
            for j in range(NB):
                x_ref[at, j * BLK : (j + 1) * BLK] = messages[4 * h + t][pl.ds(j, MSG_ROWS, stride=NB), :]


def split(value):
    hi = value.astype(bf16)
    return hi, (value - hi.astype(f32)).astype(bf16)


def dot(left, right):
    return jnp.dot(left, right, preferred_element_type=f32)


def block_index(i, j):
    return i * NB - i * (i - 1) // 2 + (j - i)


def rows(start, size):
    return pl.ds(pl.multiple_of(start, 8), size)


def gram_kernel(place_ref, *refs):
    messages, keeps, gives = refs[:8], refs[8:12], refs[12:16]
    x_ref, hi_ref, lo_ref, hit_ref, lot_ref, gram_ref = refs[16:]
    gather_rows(messages, x_ref)
    hi, lo = split(x_ref[...])
    hi_ref[...] = hi
    lo_ref[...] = lo
    hit_ref[...] = hi_ref[...].T
    lot_ref[...] = lo_ref[...].T
    for p in range(NT):
        r = slice(p * TILE, (p + 1) * TILE)
        w = slice(p * TILE, C)
        acc = dot(hit_ref[r, :], hi_ref[:, w])
        acc = acc + dot(hit_ref[r, :], lo_ref[:, w])
        acc = acc + dot(lot_ref[r, :], hi_ref[:, w])
        for i in (2 * p, 2 * p + 1):
            for j in range(i, NB):
                b = block_index(i, j)
                gram_ref[b * BLK : (b + 1) * BLK, :] = acc[
                    (i - 2 * p) * BLK : (i - 2 * p + 1) * BLK, (j - 2 * p) * BLK : (j - 2 * p + 1) * BLK
                ]
    z, core = place_ref[2], place_ref[3]
    for outs, c in ((keeps, core), (gives, 1 - core)):
        way = 1 - 2 * c
        for i in (1, 2, 3):
            d = (z + way * i) & 7
            outs[i - 1][:HALF, :] = gram_ref[rows(d * PART + c * HALF, HALF), :]
            outs[i - 1][HALF:, :] = gram_ref[rows(d * PART + (1 - c) * HALF, HALF), :]
        d = (z + 4) & 7
        outs[3][:HALF, :] = gram_ref[rows(d * PART + c * HALF, HALF), :]
        outs[3][HALF:, :] = gram_ref[rows(z * PART + c * HALF, HALF), :]


def diagonal(p, width):
    row = lax.broadcasted_iota(jnp.int32, (TILE, width), 0)
    col = lax.broadcasted_iota(jnp.int32, (TILE, width), 1)
    return row == col


def put(p, value, h_ref, l_ref):
    hi, lo = split(value)
    r = slice(p * TILE, (p + 1) * TILE)
    h_ref[r, p * TILE :] = hi
    l_ref[r, p * TILE :] = lo
    for q in range(p + 1, NT):
        w = slice((q - p) * TILE, (q - p + 1) * TILE)
        h_ref[q * TILE : (q + 1) * TILE, r] = hi[:, w].T
        l_ref[q * TILE : (q + 1) * TILE, r] = lo[:, w].T


def product_row(r, w, left, right):
    acc = dot(left[0][r, :], right[0][:, w])
    acc = acc + dot(left[0][r, :], right[1][:, w])
    return acc + dot(left[1][r, :], right[0][:, w])


def polynomial(s, out):
    for p in range(NT):
        r = slice(p * TILE, (p + 1) * TILE)
        w = slice(p * TILE, C)
        acc = third_coef * product_row(r, w, s, s)
        acc = acc + second_coef * (s[0][r, w].astype(f32) + s[1][r, w].astype(f32))
        acc = acc + jnp.where(diagonal(p, C - p * TILE), first_coef, 0.0)
        put(p, acc, out[0], out[1])


def symmetric_product(left, right, out):
    for p in range(NT):
        r = slice(p * TILE, (p + 1) * TILE)
        put(p, product_row(r, slice(p * TILE, C), left, right), out[0], out[1])


def step_kernel(place_ref, own, g1, g2, g3, g4, n1, n2, n3, n4, *refs):
    messages, outs = refs[:8], refs[8:16]
    gram_ref, x_ref, ah, al, bh, bl, ch, cl, xh, xl = refs[16:]
    z, core = place_ref[2], place_ref[3]
    far = (z + 4) & 7
    gram_ref[rows(z * PART + core * HALF, HALF), :] = own[:HALF, :]
    gram_ref[rows(z * PART + (1 - core) * HALF, HALF), :] = own[HALF:, :]
    gram_ref[rows(far * PART + core * HALF, HALF), :] = g4[...]
    gram_ref[rows(far * PART + (1 - core) * HALF, HALF), :] = n4[...]
    for c, parts in ((core, (g1, g2, g3)), (1 - core, (n1, n2, n3))):
        way = 1 - 2 * c
        for i, part in enumerate(parts):
            d = (z - way * (i + 1)) & 7
            gram_ref[rows(d * PART + c * HALF, HALF), :] = part[:HALF, :]
            gram_ref[rows(d * PART + (1 - c) * HALF, HALF), :] = part[HALF:, :]
    row = lax.broadcasted_iota(jnp.int32, (BLK, BLK), 0)
    col = lax.broadcasted_iota(jnp.int32, (BLK, BLK), 1)
    diag = jnp.zeros((BLK, BLK), f32)
    for i in range(NB):
        b = block_index(i, i)
        diag = diag + gram_ref[b * BLK : (b + 1) * BLK, :]
    diag = jnp.where(row == col, diag, 0.0)
    total = jnp.sum(jnp.sum(diag, axis=0, keepdims=True), axis=1, keepdims=True)
    inverse = 1.0 / (jnp.sqrt(total) + norm_epsilon)
    for i in range(NB):
        for j in range(i, NB):
            b = block_index(i, j)
            hi, lo = split(gram_ref[b * BLK : (b + 1) * BLK, :] * inverse * inverse)
            ri = slice(i * BLK, (i + 1) * BLK)
            rj = slice(j * BLK, (j + 1) * BLK)
            ah[ri, rj] = hi
            al[ri, rj] = lo
            if j > i:
                ah[rj, ri] = hi.T
                al[rj, ri] = lo.T
    gather_rows(messages, x_ref)
    hi, lo = split(x_ref[...])
    xh[...] = hi
    xl[...] = lo
    polynomial((ah, al), (bh, bl))
    everything = slice(0, C)
    bands = [slice(t * BAND, (t + 1) * BAND) for t in range(4)]
    for at in bands:
        x_ref[at, :] = product_row(at, everything, (xh, xl), (bh, bl))
    symmetric_product((ah, al), (bh, bl), (ch, cl))
    symmetric_product((ch, cl), (bh, bl), (ah, al))
    for at in bands:
        hi, lo = split(x_ref[at, :])
        xh[at, :] = hi
        xl[at, :] = lo
    factor = inverse * out_scale
    for at in bands:
        inner = third_coef * product_row(at, everything, (xh, xl), (ah, al)) + second_coef * x_ref[at, :]
        hi, lo = split(inner)
        xh[at, :] = hi
        xl[at, :] = lo
    for i, at in enumerate(bands):
        result = product_row(at, everything, (xh, xl), (ah, al)) + first_coef * x_ref[at, :]
        result = result * factor
        for e in range(2):
            out_ref = outs[2 * i + e]
            for j in range(NB):
                out_ref[pl.ds(j, MSG_ROWS, stride=NB), :] = result[
                    e * MSG_ROWS : (e + 1) * MSG_ROWS, j * BLK : (j + 1) * BLK
                ]


def update_kernel(table_ref, place_ref, *refs):
    ins, (update_ref, chosen_ref) = refs[:8], refs[8:]
    fill_chosen(table_ref, place_ref, chosen_ref)
    for k in range(MATS):

        @pl.when(table_ref[k] >= GROUPS)
        def _():
            update_ref[k] = jnp.zeros((2 * LINES, BLK), f32)

    for slot in range(GROUPS):
        s, t = slot // 4, slot % 4
        k = chosen_ref[slot]
        for h in range(2):
            update_ref[k, h * LINES : (h + 1) * LINES, :] = ins[4 * h + s][t * LINES : (t + 1) * LINES, :]


VMEM = pl.BlockSpec(memory_space=pltpu.VMEM)
SMEM = pl.BlockSpec(memory_space=pltpu.SMEM)
HBM = pl.BlockSpec(memory_space=pl.ANY)


def shape(*dims):
    return jax.ShapeDtypeStruct(dims, f32)


def call(kernel, in_specs, out_shape, scratch, name, flops, moved, mib):
    return pl.pallas_call(
        kernel,
        in_specs=in_specs,
        out_specs=jax.tree.map(lambda _: VMEM, out_shape),
        out_shape=out_shape,
        scratch_shapes=scratch,
        name=name,
        cost_estimate=pl.CostEstimate(flops=flops, bytes_accessed=moved, transcendentals=0),
        compiler_params=pltpu.CompilerParams(vmem_limit_bytes=mib * 1024 * 1024),
    )


MESSAGES = [shape(MSG_LINES, BLK)] * 4
MSG_BYTES = 8 * MSG_LINES * BLK * 4


def exchange(messages, regroup, outward):
    first, second = (first_axis, second_axis) if outward else (second_axis, first_axis)
    sign = 1 if outward else -1
    middle = [messages[0]] + [permute(messages[s], first(sign * s)) for s in (1, 2, 3)]
    middle = regroup(*middle)
    return [middle[0]] + [permute(middle[t], second(sign * t)) for t in (1, 2, 3)]


def shards(grads, momentum, owner_table):
    grp, row = lax.axis_index("grp"), lax.axis_index("row")
    core = row % 2
    place = jnp.stack([(row // 2) % 4, grp % 4, (grp // 4) * 2 + row // 8, core]).astype(jnp.int32)
    lines = (MATS, 2 * LINES, BLK)
    grads, momentum = grads.reshape(lines), momentum.reshape(lines)

    outgoing = call(
        outgoing_kernel, [SMEM, SMEM, HBM, HBM], MESSAGES * 2,
        [
            pltpu.SMEM((GROUPS,), jnp.int32),
            pltpu.VMEM((GROUPS, 2 * LINES, BLK), f32),
            pltpu.VMEM((GROUPS, 2 * LINES, BLK), f32),
            pltpu.SemaphoreType.DMA((2, GROUPS)),
        ],
        "outgoing", 0, 3 * MSG_BYTES, 10,
    )(owner_table, place, grads, momentum)

    regroup = call(regroup_kernel, [VMEM] * 4, MESSAGES, [], "regroup", 0, MSG_BYTES, 4)
    owned = exchange(outgoing[:4], regroup, True) + exchange(outgoing[4:], regroup, True)

    mom_spec = pl.BlockSpec((MOM_STEP, 2 * LINES, BLK), lambda i: (i, 0, 0))
    new_momentum = pl.pallas_call(
        momentum_kernel,
        grid=(MATS // MOM_STEP,),
        in_specs=[SMEM, mom_spec, mom_spec],
        out_specs=mom_spec,
        out_shape=shape(*lines),
        name="momentum",
        cost_estimate=pl.CostEstimate(flops=0, bytes_accessed=12 * MATS * 2 * LINES * BLK, transcendentals=0),
    )(owner_table, grads, momentum)

    tall = [pltpu.VMEM((8 * MSG_ROWS, C), bf16)] * 2
    whole = pltpu.VMEM((8 * MSG_ROWS, C), f32)
    triangle = pltpu.VMEM((TRI * BLK, BLK), f32)
    sums = call(
        gram_kernel, [SMEM] + [VMEM] * 8, [shape(PART, BLK)] * 8,
        [whole] + tall + [pltpu.VMEM((C, 8 * MSG_ROWS), bf16)] * 2 + [triangle],
        "gram", 3 * 8 * MSG_ROWS * C * C, MSG_BYTES + 8 * PART * BLK * 4, 20,
    )(place, *owned)
    keeps, gives = sums[:4], sums[4:]

    chip = [keep + swap_cores(give) for keep, give in zip(keeps, gives)]
    near, middle, distant = chip[:3]
    farthest, mine = chip[3][:HALF], chip[3][HALF:]
    from_distant, from_farthest = along_z(distant, 1), along_z(farthest, 2)
    from_near = along_z(near, 1)
    middle = middle + from_distant
    middle = jnp.concatenate([middle[:HALF] + from_farthest, middle[HALF:]])
    moving = from_near + along_z(middle, 2)
    moving = jnp.concatenate([moving[:HALF] + mine, moving[HALF:]])
    other = swap_cores(moving)
    own = jnp.concatenate([moving[:HALF] + other[HALF:], moving[HALF:] + other[:HALF]])

    g2 = along_z(own, 2)
    g1 = along_z(own, 1)
    g3 = along_z(g2, 1)
    g4 = along_z(g2[:HALF], 2)
    n1, n2, n3, n4 = swap_cores(g1), swap_cores(g2), swap_cores(g3), swap_cores(g4)

    results = call(
        step_kernel, [SMEM] + [VMEM] * 17, MESSAGES * 2,
        [triangle, whole] + [pltpu.VMEM((C, C), bf16)] * 6 + tall,
        "newton", 6 * (3 * C * C * C * 5 // 8 + 3 * 8 * MSG_ROWS * C * C), 2 * MSG_BYTES + 4 * TRI * BLK * BLK, 36,
    )(place, own, g1, g2, g3, g4, n1, n2, n3, n4, *owned)

    back = exchange(results[:4], regroup, False) + exchange(results[4:], regroup, False)
    update = call(
        update_kernel, [SMEM, SMEM] + [VMEM] * 8, shape(*lines),
        [pltpu.SMEM((GROUPS,), jnp.int32)], "update", 0, 2 * MSG_BYTES, 10,
    )(owner_table, place, *back)
    state = (MATS, 1, 2 * LINES * BLK // C, C)
    return (new_momentum.reshape(state), update.reshape(state))


def solution(mesh):
    in_specs = (P(None, "row", "grp", None), P(None, "row", "grp", None), P())
    out_specs = (P(None, "row", "grp", None), P(None, "row", "grp", None))
    return jax.shard_map(shards, mesh=mesh, in_specs=in_specs, out_specs=out_specs, check_vma=False)
```

```python
import functools
import math

import jax
import jax.numpy as jnp
from jax import lax
from jax.experimental import pallas as pl
from jax.experimental.pallas import tpu as pltpu
from jax.sharding import PartitionSpec as P

MATS = 24
GROUPS = 16
C = 1024
PIECE_ROWS = 14
LINES = PIECE_ROWS * C // 128
MSG_ROWS = 4 * PIECE_ROWS
MSG_LINES = 4 * LINES
BAND = 2 * MSG_ROWS
MOM_STEP = 4
ROWS = 7168
TILE = 256
NT = C // TILE
BLK = 128
NB = C // BLK
TRI = NB * (NB + 1) // 2
PART = TRI * BLK // 8
HALF = PART // 2

momentum_decay = 0.95
norm_epsilon = 1e-07
first_coef = 3.4445
second_coef = -4.775
third_coef = 2.0315
out_scale = 0.2 * math.sqrt(max(ROWS, C))

f32 = jnp.float32
bf16 = jnp.bfloat16
ALL = ("grp", "row")


def coords(n):
    core = n % 2
    x = (n // 2) % 4
    z_lo = (n // 8) % 2
    y = (n // 16) % 4
    z_hi = n // 64
    return (x, y, z_hi * 2 + z_lo, core)


def number(x, y, z, core):
    return ((((z // 2) * 4 + y) * 2 + z % 2) * 4 + x) * 2 + core


def pairs(move):
    out = []
    for n in range(256):
        x, y, z, core = coords(n)
        out.append((n, number(*move(x, y, z, core))))
    return out


def first_axis(step):
    return pairs(
        lambda x, y, z, c: ((x + step) % 4, y, z, c) if c == 0 else (x, (y + step) % 4, z, c)
    )


def second_axis(step):
    return pairs(
        lambda x, y, z, c: (x, (y + step) % 4, z, c) if c == 0 else ((x + step) % 4, y, z, c)
    )


def permute(value, perm):
    return lax.ppermute(value, ALL, perm)


def swap_cores(value):
    return permute(value, pairs(lambda x, y, z, c: (x, y, z, 1 - c)))


def along_z(value, step):
    return permute(value, pairs(lambda x, y, z, c: (x, y, (z + step * (1 - 2 * c)) % 8, c)))


def fill_chosen(table_ref, place_ref, chosen_ref):
    x, y, core = place_ref[0], place_ref[1], place_ref[3]
    for k in range(MATS):
        owner = table_ref[k]

        @pl.when(owner < GROUPS)
        def _():
            dx = ((owner & 3) - x) & 3
            dy = ((owner >> 2) - y) & 3
            slot = jnp.where(core == 0, dx * 4 + dy, dy * 4 + dx)
            chosen_ref[slot] = k


def outgoing_kernel(half, table_ref, place_ref, grads_ref, mom_ref, o0, o1, o2, o3, chosen_ref, gbuf, mbuf, sems):
    lines = pl.ds(half * LINES, LINES)
    grads_copy = pltpu.make_async_copy(grads_ref.at[:, lines], gbuf, sems.at[0])
    mom_copy = pltpu.make_async_copy(mom_ref.at[:, lines], mbuf, sems.at[1])
    grads_copy.start()
    mom_copy.start()
    fill_chosen(table_ref, place_ref, chosen_ref)
    grads_copy.wait()
    mom_copy.wait()
    outs = (o0, o1, o2, o3)
    for slot in range(GROUPS):
        k = chosen_ref[slot]
        g = gbuf[k]
        new = momentum_decay * mbuf[k] + g
        t = slot % 4
        outs[slot // 4][t * LINES : (t + 1) * LINES, :] = g + momentum_decay * new


def momentum_kernel(table_ref, grads_ref, mom_ref, new_ref):
    for i in range(MOM_STEP):
        k = pl.program_id(0) * MOM_STEP + i
        m = mom_ref[i]
        new_ref[i] = jnp.where(table_ref[k] < GROUPS, momentum_decay * m + grads_ref[i], m)


def regroup_kernel(i0, i1, i2, i3, o0, o1, o2, o3):
    ins, outs = (i0, i1, i2, i3), (o0, o1, o2, o3)
    for t in range(4):
        for s in range(4):
            outs[t][s * LINES : (s + 1) * LINES, :] = ins[s][t * LINES : (t + 1) * LINES, :]


def gather_rows(messages, x_ref):
    for h in range(2):
        for t in range(4):
            at = slice((h * 4 + t) * MSG_ROWS, (h * 4 + t + 1) * MSG_ROWS)
            for j in range(NB):
                x_ref[at, j * BLK : (j + 1) * BLK] = messages[4 * h + t][pl.ds(j, MSG_ROWS, stride=NB), :]


def split(value):
    hi = value.astype(bf16)
    return hi, (value - hi.astype(f32)).astype(bf16)


def dot(left, right):
    return jnp.dot(left, right, preferred_element_type=f32)


def block_index(i, j):
    return i * NB - i * (i - 1) // 2 + (j - i)


def rows(start, size):
    return pl.ds(pl.multiple_of(start, 8), size)


def gram_kernel(place_ref, *refs):
    messages, keeps, gives = refs[:8], refs[8:12], refs[12:16]
    x_ref, hi_ref, lo_ref, hit_ref, lot_ref, gram_ref = refs[16:]
    gather_rows(messages, x_ref)
    hi, lo = split(x_ref[...])
    hi_ref[...] = hi
    lo_ref[...] = lo
    hit_ref[...] = hi_ref[...].T
    lot_ref[...] = lo_ref[...].T
    for p in range(NT):
        r = slice(p * TILE, (p + 1) * TILE)
        w = slice(p * TILE, C)
        acc = dot(hit_ref[r, :], hi_ref[:, w])
        acc = acc + dot(hit_ref[r, :], lo_ref[:, w])
        acc = acc + dot(lot_ref[r, :], hi_ref[:, w])
        for i in (2 * p, 2 * p + 1):
            for j in range(i, NB):
                b = block_index(i, j)
                gram_ref[b * BLK : (b + 1) * BLK, :] = acc[
                    (i - 2 * p) * BLK : (i - 2 * p + 1) * BLK, (j - 2 * p) * BLK : (j - 2 * p + 1) * BLK
                ]
    z, core = place_ref[2], place_ref[3]
    for outs, c in ((keeps, core), (gives, 1 - core)):
        way = 1 - 2 * c
        for i in (1, 2, 3):
            d = (z + way * i) & 7
            outs[i - 1][:HALF, :] = gram_ref[rows(d * PART + c * HALF, HALF), :]
            outs[i - 1][HALF:, :] = gram_ref[rows(d * PART + (1 - c) * HALF, HALF), :]
        d = (z + 4) & 7
        outs[3][:HALF, :] = gram_ref[rows(d * PART + c * HALF, HALF), :]
        outs[3][HALF:, :] = gram_ref[rows(z * PART + c * HALF, HALF), :]


def diagonal(width):
    row = lax.broadcasted_iota(jnp.int32, (TILE, width), 0)
    col = lax.broadcasted_iota(jnp.int32, (TILE, width), 1)
    return row == col


def tile(p):
    return slice(p * TILE, (p + 1) * TILE)


def put(p, value, out):
    hi, lo = split(value)
    out[0][tile(p), p * TILE :] = hi
    out[1][tile(p), p * TILE :] = lo
    for q in range(p + 1, NT):
        out[0][tile(q), tile(p)] = hi[:, tile(q - p)].T
        out[1][tile(q), tile(p)] = lo[:, tile(q - p)].T


def product(r, w, left, right):
    acc = dot(left[0][r, :], right[0][:, w])
    acc = acc + dot(left[0][r, :], right[1][:, w])
    return acc + dot(left[1][r, :], right[0][:, w])


def polynomial(s, out):
    for p in range(NT):
        r, w = tile(p), slice(p * TILE, C)
        acc = third_coef * product(r, w, s, s)
        acc = acc + second_coef * (s[0][r, w].astype(f32) + s[1][r, w].astype(f32))
        put(p, acc + jnp.where(diagonal(C - p * TILE), first_coef, 0.0), out)


def symmetric_product(left, right, out):
    for p in range(NT):
        put(p, product(tile(p), slice(p * TILE, C), left, right), out)


def step_kernel(place_ref, own, g1, g2, g3, g4, n1, n2, n3, n4, *refs):
    messages, outs = refs[:8], refs[8:16]
    gram_ref, x_ref, y_ref, ah, al, bh, bl, ch, cl, xh, xl = refs[16:]
    z, core = place_ref[2], place_ref[3]
    far = (z + 4) & 7
    gram_ref[rows(z * PART + core * HALF, HALF), :] = own[:HALF, :]
    gram_ref[rows(z * PART + (1 - core) * HALF, HALF), :] = own[HALF:, :]
    gram_ref[rows(far * PART + core * HALF, HALF), :] = g4[...]
    gram_ref[rows(far * PART + (1 - core) * HALF, HALF), :] = n4[...]
    for c, parts in ((core, (g1, g2, g3)), (1 - core, (n1, n2, n3))):
        way = 1 - 2 * c
        for i, part in enumerate(parts):
            d = (z - way * (i + 1)) & 7
            gram_ref[rows(d * PART + c * HALF, HALF), :] = part[:HALF, :]
            gram_ref[rows(d * PART + (1 - c) * HALF, HALF), :] = part[HALF:, :]
    row = lax.broadcasted_iota(jnp.int32, (BLK, BLK), 0)
    col = lax.broadcasted_iota(jnp.int32, (BLK, BLK), 1)
    diag = jnp.zeros((BLK, BLK), f32)
    for i in range(NB):
        b = block_index(i, i)
        diag = diag + gram_ref[b * BLK : (b + 1) * BLK, :]
    diag = jnp.where(row == col, diag, 0.0)
    total = jnp.sum(jnp.sum(diag, axis=0, keepdims=True), axis=1, keepdims=True)
    inverse = 1.0 / (jnp.sqrt(total) + norm_epsilon)
    for i in range(NB):
        for j in range(i, NB):
            b = block_index(i, j)
            block = gram_ref[b * BLK : (b + 1) * BLK, :] * inverse * inverse
            ri = slice(i * BLK, (i + 1) * BLK)
            rj = slice(j * BLK, (j + 1) * BLK)
            hi, lo = split(block)
            ah[ri, rj], al[ri, rj] = hi, lo
            if j > i:
                ah[rj, ri], al[rj, ri] = hi.T, lo.T
    gather_rows(messages, x_ref)
    hi, lo = split(x_ref[...])
    xh[...] = hi
    xl[...] = lo
    polynomial((ah, al), (bh, bl))
    everything = slice(0, 8 * MSG_ROWS)
    columns = [tile(q) for q in range(NT)]
    for w in columns:
        y_ref[:, w] = product(everything, w, (xh, xl), (bh, bl))
    symmetric_product((ah, al), (bh, bl), (ch, cl))
    symmetric_product((ch, cl), (bh, bl), (ah, al))
    hi, lo = split(y_ref[...])
    xh[...] = hi
    xl[...] = lo
    for w in columns:
        x_ref[:, w] = third_coef * product(everything, w, (xh, xl), (ah, al)) + second_coef * y_ref[:, w]
    hi, lo = split(x_ref[...])
    xh[...] = hi
    xl[...] = lo
    factor = inverse * out_scale
    for q, w in enumerate(columns):
        result = (product(everything, w, (xh, xl), (ah, al)) + first_coef * y_ref[:, w]) * factor
        for i, out_ref in enumerate(outs):
            for j in range(TILE // BLK):
                out_ref[pl.ds(q * (TILE // BLK) + j, MSG_ROWS, stride=NB), :] = result[
                    i * MSG_ROWS : (i + 1) * MSG_ROWS, j * BLK : (j + 1) * BLK
                ]


def update_kernel(half, table_ref, place_ref, i0, i1, i2, i3, *refs):
    update_ref, chosen_ref, zero_ref, sems = refs[-4:]
    lines = pl.ds(half * LINES, LINES)
    zero_ref[...] = jnp.zeros((LINES, BLK), f32)
    fill_chosen(table_ref, place_ref, chosen_ref)

    def piece_copy(slot):
        source = (i0, i1, i2, i3)[slot // 4].at[pl.ds(slot % 4 * LINES, LINES)]
        return pltpu.make_async_copy(source, update_ref.at[chosen_ref[slot], lines], sems.at[slot])

    def zero_copy(k):
        return pltpu.make_async_copy(zero_ref, update_ref.at[k, lines], sems.at[GROUPS + k])

    for slot in range(GROUPS):
        piece_copy(slot).start()
    for k in range(MATS):
        pl.when(table_ref[k] >= GROUPS)(lambda k=k: zero_copy(k).start())
    for slot in range(GROUPS):
        piece_copy(slot).wait()
    for k in range(MATS):
        pl.when(table_ref[k] >= GROUPS)(lambda k=k: zero_copy(k).wait())


VMEM = pl.BlockSpec(memory_space=pltpu.VMEM)
SMEM = pl.BlockSpec(memory_space=pltpu.SMEM)
HBM = pl.BlockSpec(memory_space=pltpu.HBM)


def shape(*dims):
    return jax.ShapeDtypeStruct(dims, f32)


def call(kernel, in_specs, out_shape, scratch, name, flops, moved, mib, out_spec=VMEM, aliases={}):
    return pl.pallas_call(
        kernel,
        in_specs=in_specs,
        out_specs=jax.tree.map(lambda _: out_spec, out_shape),
        input_output_aliases=aliases,
        out_shape=out_shape,
        scratch_shapes=scratch,
        name=name,
        cost_estimate=pl.CostEstimate(flops=flops, bytes_accessed=moved, transcendentals=0),
        compiler_params=pltpu.CompilerParams(vmem_limit_bytes=mib * 1024 * 1024),
    )


MESSAGES = [shape(MSG_LINES, BLK)] * 4
MSG_BYTES = 8 * MSG_LINES * BLK * 4


def exchange(messages, regroup, outward):
    first, second = (first_axis, second_axis) if outward else (second_axis, first_axis)
    sign = 1 if outward else -1
    middle = [messages[0]] + [permute(messages[s], first(sign * s)) for s in (1, 2, 3)]
    middle = regroup(*middle)
    return [middle[0]] + [permute(middle[t], second(sign * t)) for t in (1, 2, 3)]


def shards(grads, momentum, owner_table):
    grp, row = lax.axis_index("grp"), lax.axis_index("row")
    core = row % 2
    place = jnp.stack([(row // 2) % 4, grp % 4, (grp // 4) * 2 + row // 8, core]).astype(jnp.int32)
    lines = (MATS, 2 * LINES, BLK)
    grads, momentum = grads.reshape(lines), momentum.reshape(lines)

    outgoing = [
        call(
            functools.partial(outgoing_kernel, half), [SMEM, SMEM, HBM, HBM], MESSAGES,
            [pltpu.SMEM((GROUPS,), jnp.int32)]
            + [pltpu.VMEM((MATS, LINES, BLK), f32)] * 2
            + [pltpu.SemaphoreType.DMA((2,))],
            "outgoing", 0, 2 * MSG_BYTES, 48,
        )(owner_table, place, grads, momentum)
        for half in range(2)
    ]

    regroup = call(regroup_kernel, [VMEM] * 4, MESSAGES, [], "regroup", 0, MSG_BYTES, 4)
    owned = exchange(outgoing[0], regroup, True) + exchange(outgoing[1], regroup, True)

    tall = [pltpu.VMEM((8 * MSG_ROWS, C), bf16)] * 2
    whole = pltpu.VMEM((8 * MSG_ROWS, C), f32)
    triangle = pltpu.VMEM((TRI * BLK, BLK), f32)
    sums = call(
        gram_kernel, [SMEM] + [VMEM] * 8, [shape(PART, BLK)] * 8,
        [whole] + tall + [pltpu.VMEM((C, 8 * MSG_ROWS), bf16)] * 2 + [triangle],
        "gram", 3 * 8 * MSG_ROWS * C * C, MSG_BYTES + 8 * PART * BLK * 4, 20,
    )(place, *owned)
    keeps, gives = sums[:4], sums[4:]

    distant = keeps[2] + swap_cores(gives[2])
    ends = keeps[3] + swap_cores(gives[3])
    distant, ends, late_near, late_middle = lax.optimization_barrier((distant, ends, gives[0], gives[1]))
    near = keeps[0] + swap_cores(late_near)
    middle = keeps[1] + swap_cores(late_middle)
    farthest, mine = ends[:HALF], ends[HALF:]
    from_distant, from_farthest = along_z(distant, 1), along_z(farthest, 2)
    from_near = along_z(near, 1)
    middle = middle + from_distant
    middle = jnp.concatenate([middle[:HALF] + from_farthest, middle[HALF:]])
    moving = from_near + along_z(middle, 2)
    moving = jnp.concatenate([moving[:HALF] + mine, moving[HALF:]])
    other = swap_cores(moving)
    own = jnp.concatenate([moving[:HALF] + other[HALF:], moving[HALF:] + other[:HALF]])

    g2 = along_z(own, 2)
    g1 = along_z(own, 1)

    late_table, _ = lax.optimization_barrier((owner_table, own))
    mom_spec = pl.BlockSpec((MOM_STEP, 2 * LINES, BLK), lambda i: (i, 0, 0))
    new_momentum = pl.pallas_call(
        momentum_kernel,
        grid=(MATS // MOM_STEP,),
        in_specs=[SMEM, mom_spec, mom_spec],
        out_specs=mom_spec,
        out_shape=shape(*lines),
        name="momentum",
        cost_estimate=pl.CostEstimate(flops=0, bytes_accessed=12 * MATS * 2 * LINES * BLK, transcendentals=0),
    )(late_table, grads, momentum)
    new_momentum, g2 = lax.optimization_barrier((new_momentum, g2))

    g3 = along_z(g2, 1)
    g4 = along_z(g2[:HALF], 2)
    n1, n2, n3, n4 = swap_cores(g1), swap_cores(g2), swap_cores(g3), swap_cores(g4)

    results = call(
        step_kernel, [SMEM] + [VMEM] * 17, MESSAGES * 2,
        [triangle, whole, whole] + [pltpu.VMEM((C, C), bf16)] * 6 + tall,
        "newton", 6 * (3 * C * C * C * 5 // 8 + 3 * 8 * MSG_ROWS * C * C), 2 * MSG_BYTES + 4 * TRI * BLK * BLK, 36,
    )(place, own, g1, g2, g3, g4, n1, n2, n3, n4, *owned)

    update = []
    for half in range(2):
        back = exchange(results[4 * half : 4 * half + 4], regroup, False)
        update = [
            call(
                functools.partial(update_kernel, half), [SMEM, SMEM] + [VMEM] * 4 + [HBM] * half, shape(*lines),
                [
                    pltpu.SMEM((GROUPS,), jnp.int32),
                    pltpu.VMEM((LINES, BLK), f32),
                    pltpu.SemaphoreType.DMA((GROUPS + MATS,)),
                ],
                "update", 0, MSG_BYTES, 4, HBM, {6: 0} if half else {},
            )(owner_table, place, *back, *update)
        ]
    update = update[0]
    state = (MATS, 1, 2 * LINES * BLK // C, C)
    return (new_momentum.reshape(state), update.reshape(state))


def solution(mesh):
    in_specs = (P(None, "row", "grp", None), P(None, "row", "grp", None), P())
    out_specs = (P(None, "row", "grp", None), P(None, "row", "grp", None))
    return jax.shard_map(shards, mesh=mesh, in_specs=in_specs, out_specs=out_specs, check_vma=False)
```

```python
import functools
import math

import jax
import jax.numpy as jnp
from jax import lax
from jax.experimental import pallas as pl
from jax.experimental.pallas import tpu as pltpu
from jax.sharding import PartitionSpec as P

MATS = 24
GROUPS = 16
C = 1024
PIECE_ROWS = 14
LINES = PIECE_ROWS * C // 128
MSG_ROWS = 4 * PIECE_ROWS
MSG_LINES = 4 * LINES
BAND = 2 * MSG_ROWS
ROWS = 7168
TILE = 256
NT = C // TILE
BLK = 128
NB = C // BLK
TRI = NB * (NB + 1) // 2
PART = TRI * BLK // 8
HALF = PART // 2

momentum_decay = 0.95
norm_epsilon = 1e-07
first_coef = 3.4445
second_coef = -4.775
third_coef = 2.0315
out_scale = 0.2 * math.sqrt(max(ROWS, C))

f32 = jnp.float32
bf16 = jnp.bfloat16
ALL = ("grp", "row")


def coords(n):
    core = n % 2
    x = (n // 2) % 4
    z_lo = (n // 8) % 2
    y = (n // 16) % 4
    z_hi = n // 64
    return (x, y, z_hi * 2 + z_lo, core)


def number(x, y, z, core):
    return ((((z // 2) * 4 + y) * 2 + z % 2) * 4 + x) * 2 + core


def pairs(move):
    out = []
    for n in range(256):
        x, y, z, core = coords(n)
        out.append((n, number(*move(x, y, z, core))))
    return out


def first_axis(step):
    return pairs(
        lambda x, y, z, c: ((x + step) % 4, y, z, c) if c == 0 else (x, (y + step) % 4, z, c)
    )


def second_axis(step):
    return pairs(
        lambda x, y, z, c: (x, (y + step) % 4, z, c) if c == 0 else ((x + step) % 4, y, z, c)
    )


def permute(value, perm):
    return lax.ppermute(value, ALL, perm)


def swap_cores(value):
    return permute(value, pairs(lambda x, y, z, c: (x, y, z, 1 - c)))


def along_z(value, step):
    return permute(value, pairs(lambda x, y, z, c: (x, y, (z + step * (1 - 2 * c)) % 8, c)))


def fill_chosen(table_ref, place_ref, chosen_ref):
    x, y, core = place_ref[0], place_ref[1], place_ref[3]
    for k in range(MATS):
        owner = table_ref[k]

        @pl.when(owner < GROUPS)
        def _():
            dx = ((owner & 3) - x) & 3
            dy = ((owner >> 2) - y) & 3
            slot = jnp.where(core == 0, dx * 4 + dy, dy * 4 + dx)
            chosen_ref[slot] = k


def outgoing_kernel(half, table_ref, place_ref, grads_ref, mom_ref, chosen_ref, o0, o1, o2, o3, gbuf, mbuf, sems):
    lines = pl.ds(half * LINES, LINES)
    grads_copy = pltpu.make_async_copy(grads_ref.at[:, lines], gbuf, sems.at[0])
    mom_copy = pltpu.make_async_copy(mom_ref.at[:, lines], mbuf, sems.at[1])
    grads_copy.start()
    mom_copy.start()
    if half == 0:
        fill_chosen(table_ref, place_ref, chosen_ref)
    grads_copy.wait()
    mom_copy.wait()
    outs = (o0, o1, o2, o3)
    for slot in range(GROUPS):
        k = chosen_ref[slot]
        g = gbuf[k]
        new = momentum_decay * mbuf[k] + g
        t = slot % 4
        outs[slot // 4][t * LINES : (t + 1) * LINES, :] = g + momentum_decay * new


def momentum_kernel(table_ref, grads_ref, mom_ref, new_ref):
    for k in range(MATS):
        m = mom_ref[k]
        new_ref[k] = jnp.where(table_ref[k] < GROUPS, momentum_decay * m + grads_ref[k], m)


def regroup_kernel(i0, i1, i2, i3, o0, o1, o2, o3):
    ins, outs = (i0, i1, i2, i3), (o0, o1, o2, o3)
    for t in range(4):
        for s in range(4):
            outs[t][s * LINES : (s + 1) * LINES, :] = ins[s][t * LINES : (t + 1) * LINES, :]


def gather_rows(messages, x_ref):
    for h in range(2):
        for t in range(4):
            at = slice((h * 4 + t) * MSG_ROWS, (h * 4 + t + 1) * MSG_ROWS)
            for j in range(NB):
                x_ref[at, j * BLK : (j + 1) * BLK] = messages[4 * h + t][pl.ds(j, MSG_ROWS, stride=NB), :]


def split(value):
    hi = value.astype(bf16)
    return hi, (value - hi.astype(f32)).astype(bf16)


def dot(left, right):
    return jnp.dot(left, right, preferred_element_type=f32)


def block_index(i, j):
    return i * NB - i * (i - 1) // 2 + (j - i)


def rows(start, size):
    return pl.ds(pl.multiple_of(start, 8), size)


def gram_kernel(place_ref, *refs):
    messages, keeps, gives = refs[:8], refs[8:12], refs[12:16]
    x_ref, hi_ref, lo_ref, hit_ref, lot_ref, gram_ref = refs[16:]
    gather_rows(messages, x_ref)
    hi, lo = split(x_ref[...])
    hi_ref[...] = hi
    lo_ref[...] = lo
    hit_ref[...] = hi_ref[...].T
    lot_ref[...] = lo_ref[...].T
    for p in range(NT):
        r = slice(p * TILE, (p + 1) * TILE)
        w = slice(p * TILE, C)
        acc = dot(hit_ref[r, :], hi_ref[:, w])
        acc = acc + dot(hit_ref[r, :], lo_ref[:, w])
        acc = acc + dot(lot_ref[r, :], hi_ref[:, w])
        for i in (2 * p, 2 * p + 1):
            for j in range(i, NB):
                b = block_index(i, j)
                gram_ref[b * BLK : (b + 1) * BLK, :] = acc[
                    (i - 2 * p) * BLK : (i - 2 * p + 1) * BLK, (j - 2 * p) * BLK : (j - 2 * p + 1) * BLK
                ]
    z, core = place_ref[2], place_ref[3]
    for outs, c in ((keeps, core), (gives, 1 - core)):
        way = 1 - 2 * c
        for i in (1, 2, 3):
            d = (z + way * i) & 7
            outs[i - 1][:HALF, :] = gram_ref[rows(d * PART + c * HALF, HALF), :]
            outs[i - 1][HALF:, :] = gram_ref[rows(d * PART + (1 - c) * HALF, HALF), :]
        d = (z + 4) & 7
        outs[3][:HALF, :] = gram_ref[rows(d * PART + c * HALF, HALF), :]
        outs[3][HALF:, :] = gram_ref[rows(z * PART + c * HALF, HALF), :]


def diagonal(width):
    row = lax.broadcasted_iota(jnp.int32, (TILE, width), 0)
    col = lax.broadcasted_iota(jnp.int32, (TILE, width), 1)
    return row == col


def tile(p):
    return slice(p * TILE, (p + 1) * TILE)


def put(p, value, out):
    hi, lo = split(value)
    out[0][tile(p), p * TILE :] = hi
    out[1][tile(p), p * TILE :] = lo
    for q in range(p + 1, NT):
        out[0][tile(q), tile(p)] = hi[:, tile(q - p)].T
        out[1][tile(q), tile(p)] = lo[:, tile(q - p)].T


def product(r, w, left, right):
    acc = dot(left[0][r, :], right[0][:, w])
    acc = acc + dot(left[0][r, :], right[1][:, w])
    return acc + dot(left[1][r, :], right[0][:, w])


def polynomial(s, out):
    for p in range(NT):
        r, w = tile(p), slice(p * TILE, C)
        acc = third_coef * product(r, w, s, s)
        acc = acc + second_coef * (s[0][r, w].astype(f32) + s[1][r, w].astype(f32))
        put(p, acc + jnp.where(diagonal(C - p * TILE), first_coef, 0.0), out)


def symmetric_product(left, right, out):
    for p in range(NT):
        put(p, product(tile(p), slice(p * TILE, C), left, right), out)


def step_kernel(place_ref, *refs):
    halves, messages, outs = refs[:16], refs[16:24], refs[24:32]
    gram_ref, x_ref, y_ref, ah, al, bh, bl, ch, cl, xh, xl = refs[32:]
    z, core = place_ref[2], place_ref[3]
    gram_ref[rows(z * PART + core * HALF, HALF), :] = halves[0][...]
    gram_ref[rows(z * PART + (1 - core) * HALF, HALF), :] = halves[1][...]
    for c, parts in ((core, halves[2:9]), (1 - core, halves[9:])):
        way = 1 - 2 * c
        for i, part in enumerate(parts):
            distance, half = (i + 1, c) if i < 4 else (i - 3, 1 - c)
            d = (z - way * distance) & 7
            gram_ref[rows(d * PART + half * HALF, HALF), :] = part[...]
    row = lax.broadcasted_iota(jnp.int32, (BLK, BLK), 0)
    col = lax.broadcasted_iota(jnp.int32, (BLK, BLK), 1)
    diag = jnp.zeros((BLK, BLK), f32)
    for i in range(NB):
        b = block_index(i, i)
        diag = diag + gram_ref[b * BLK : (b + 1) * BLK, :]
    diag = jnp.where(row == col, diag, 0.0)
    total = jnp.sum(jnp.sum(diag, axis=0, keepdims=True), axis=1, keepdims=True)
    inverse = 1.0 / (jnp.sqrt(total) + norm_epsilon)
    for i in range(NB):
        for j in range(i, NB):
            b = block_index(i, j)
            block = gram_ref[b * BLK : (b + 1) * BLK, :] * inverse * inverse
            ri = slice(i * BLK, (i + 1) * BLK)
            rj = slice(j * BLK, (j + 1) * BLK)
            hi, lo = split(block)
            ah[ri, rj], al[ri, rj] = hi, lo
            if j > i:
                ah[rj, ri], al[rj, ri] = hi.T, lo.T
    gather_rows(messages, x_ref)
    hi, lo = split(x_ref[...])
    xh[...] = hi
    xl[...] = lo
    polynomial((ah, al), (bh, bl))
    everything = slice(0, 8 * MSG_ROWS)
    columns = [tile(q) for q in range(NT)]
    for w in columns:
        y_ref[:, w] = product(everything, w, (xh, xl), (bh, bl))
    symmetric_product((ah, al), (bh, bl), (ch, cl))
    symmetric_product((ch, cl), (bh, bl), (ah, al))
    hi, lo = split(y_ref[...])
    xh[...] = hi
    xl[...] = lo
    for w in columns:
        x_ref[:, w] = third_coef * product(everything, w, (xh, xl), (ah, al)) + second_coef * y_ref[:, w]
    hi, lo = split(x_ref[...])
    xh[...] = hi
    xl[...] = lo
    factor = inverse * out_scale
    for q, w in enumerate(columns):
        result = (product(everything, w, (xh, xl), (ah, al)) + first_coef * y_ref[:, w]) * factor
        for i, out_ref in enumerate(outs):
            for j in range(TILE // BLK):
                out_ref[pl.ds(q * (TILE // BLK) + j, MSG_ROWS, stride=NB), :] = result[
                    i * MSG_ROWS : (i + 1) * MSG_ROWS, j * BLK : (j + 1) * BLK
                ]


def update_kernel(half, table_ref, chosen_ref, i0, i1, i2, i3, *refs):
    update_ref, zero_ref, sems = refs[-3:]
    lines = pl.ds(half * LINES, LINES)
    zero_ref[...] = jnp.zeros((LINES, BLK), f32)

    def piece_copy(slot):
        source = (i0, i1, i2, i3)[slot // 4].at[pl.ds(slot % 4 * LINES, LINES)]
        return pltpu.make_async_copy(source, update_ref.at[chosen_ref[slot], lines], sems.at[slot])

    def zero_copy(k):
        return pltpu.make_async_copy(zero_ref, update_ref.at[k, lines], sems.at[GROUPS + k])

    for slot in range(GROUPS):
        piece_copy(slot).start()
    for k in range(MATS):
        pl.when(table_ref[k] >= GROUPS)(lambda k=k: zero_copy(k).start())
    for slot in range(GROUPS):
        piece_copy(slot).wait()
    for k in range(MATS):
        pl.when(table_ref[k] >= GROUPS)(lambda k=k: zero_copy(k).wait())


VMEM = pl.BlockSpec(memory_space=pltpu.VMEM)
SMEM = pl.BlockSpec(memory_space=pltpu.SMEM)
HBM = pl.BlockSpec(memory_space=pltpu.HBM)


def shape(*dims):
    return jax.ShapeDtypeStruct(dims, f32)


def call(kernel, in_specs, out_shape, scratch, name, flops, moved, mib, out_specs=None, aliases={}):
    return pl.pallas_call(
        kernel,
        in_specs=in_specs,
        out_specs=out_specs or jax.tree.map(lambda _: VMEM, out_shape),
        input_output_aliases=aliases,
        out_shape=out_shape,
        scratch_shapes=scratch,
        name=name,
        cost_estimate=pl.CostEstimate(flops=flops, bytes_accessed=moved, transcendentals=0),
        compiler_params=pltpu.CompilerParams(vmem_limit_bytes=mib * 1024 * 1024),
    )


MESSAGES = [shape(MSG_LINES, BLK)] * 4
MSG_BYTES = 8 * MSG_LINES * BLK * 4


def exchange(messages, regroup, outward):
    first, second = (first_axis, second_axis) if outward else (second_axis, first_axis)
    sign = 1 if outward else -1
    middle = [messages[0]] + [permute(messages[s], first(sign * s)) for s in (1, 2, 3)]
    middle = regroup(*middle)
    return [middle[0]] + [permute(middle[t], second(sign * t)) for t in (1, 2, 3)]


def shards(grads, momentum, owner_table):
    grp, row = lax.axis_index("grp"), lax.axis_index("row")
    core = row % 2
    place = jnp.stack([(row // 2) % 4, grp % 4, (grp // 4) * 2 + row // 8, core]).astype(jnp.int32)
    lines = (MATS, 2 * LINES, BLK)
    grads, momentum = grads.reshape(lines), momentum.reshape(lines)

    buffers = [pltpu.VMEM((MATS, LINES, BLK), f32)] * 2 + [pltpu.SemaphoreType.DMA((2,))]
    chosen, *first_rows = call(
        functools.partial(outgoing_kernel, 0), [SMEM, SMEM, HBM, HBM],
        [jax.ShapeDtypeStruct((GROUPS,), jnp.int32)] + MESSAGES, buffers,
        "outgoing", 0, 2 * MSG_BYTES, 48, [SMEM] + [VMEM] * 4,
    )(owner_table, place, grads, momentum)
    last_rows = call(
        functools.partial(outgoing_kernel, 1), [SMEM, SMEM, HBM, HBM, SMEM], MESSAGES, buffers,
        "outgoing", 0, 2 * MSG_BYTES, 48,
    )(owner_table, place, grads, momentum, chosen)

    regroup = call(regroup_kernel, [VMEM] * 4, MESSAGES, [], "regroup", 0, MSG_BYTES, 4)
    owned = exchange(first_rows, regroup, True) + exchange(last_rows, regroup, True)

    tall = [pltpu.VMEM((8 * MSG_ROWS, C), bf16)] * 2
    whole = pltpu.VMEM((8 * MSG_ROWS, C), f32)
    triangle = pltpu.VMEM((TRI * BLK, BLK), f32)
    sums = call(
        gram_kernel, [SMEM] + [VMEM] * 8, [shape(PART, BLK)] * 8,
        [whole] + tall + [pltpu.VMEM((C, 8 * MSG_ROWS), bf16)] * 2 + [triangle],
        "gram", 3 * 8 * MSG_ROWS * C * C, MSG_BYTES + 8 * PART * BLK * 4, 20,
    )(place, *owned)
    keeps, gives = sums[:4], sums[4:]

    distant = keeps[2] + swap_cores(gives[2])
    ends = keeps[3] + swap_cores(gives[3])
    distant, ends, late_near, late_middle = lax.optimization_barrier((distant, ends, gives[0], gives[1]))
    near = keeps[0] + swap_cores(late_near)
    middle = keeps[1] + swap_cores(late_middle)
    moved = [middle[:HALF] + along_z(ends[:HALF], 2) + along_z(distant[:HALF], 1)]
    moved.append(middle[HALF:] + along_z(distant[HALF:], 1))
    moved = [along_z(moved[h], 2) + along_z(near[h * HALF : (h + 1) * HALF], 1) for h in range(2)]
    moved[0] = moved[0] + ends[HALF:]
    own = [moved[0] + swap_cores(moved[1]), moved[1] + swap_cores(moved[0])]

    second = [along_z(half, 2) for half in own]
    first = [along_z(half, 1) for half in own]

    late_table, _ = lax.optimization_barrier((owner_table, own[0]))
    new_momentum = call(
        momentum_kernel, [SMEM, VMEM, VMEM], shape(*lines), [], "momentum", 0, 6 * MSG_BYTES, 12,
    )(late_table, grads, momentum)
    new_momentum, second[1] = lax.optimization_barrier((new_momentum, second[1]))

    third = [along_z(half, 1) for half in second]
    fourth = along_z(second[0], 2)
    gathered = [first[0], second[0], third[0], fourth, first[1], second[1], third[1]]
    halves = own + gathered + [swap_cores(half) for half in gathered]

    results = call(
        step_kernel, [SMEM] + [VMEM] * 24, MESSAGES * 2,
        [triangle, whole, whole] + [pltpu.VMEM((C, C), bf16)] * 6 + tall,
        "newton", 6 * (3 * C * C * C * 5 // 8 + 3 * 8 * MSG_ROWS * C * C), 2 * MSG_BYTES + 4 * TRI * BLK * BLK, 36,
    )(place, *halves, *owned)

    update = []
    for half in range(2):
        back = exchange(results[4 * half : 4 * half + 4], regroup, False)
        update = [
            call(
                functools.partial(update_kernel, half), [SMEM, SMEM] + [VMEM] * 4 + [HBM] * half, shape(*lines),
                [pltpu.VMEM((LINES, BLK), f32), pltpu.SemaphoreType.DMA((GROUPS + MATS,))],
                "update", 0, MSG_BYTES, 4, HBM, {6: 0} if half else {},
            )(owner_table, chosen, *back, *update)
        ]
    update = update[0]
    state = (MATS, 1, 2 * LINES * BLK // C, C)
    return (new_momentum.reshape(state), update.reshape(state))


def solution(mesh):
    in_specs = (P(None, "row", "grp", None), P(None, "row", "grp", None), P())
    out_specs = (P(None, "row", "grp", None), P(None, "row", "grp", None))
    return jax.shard_map(shards, mesh=mesh, in_specs=in_specs, out_specs=out_specs, check_vma=False)
```

```python
import functools
import math

import jax
import jax.numpy as jnp
from jax import lax
from jax.experimental import pallas as pl
from jax.experimental.pallas import tpu as pltpu
from jax.sharding import PartitionSpec as P

MATS = 24
GROUPS = 16
C = 1024
PIECE_ROWS = 28
LINES = PIECE_ROWS * C // 128
MSG_ROWS = 2 * PIECE_ROWS
MSG_LINES = 2 * LINES
GROUP_A = 3
GROUP_B = 2
ROWS = 7168
TILE = 256
NT = C // TILE
BLK = 128
NB = C // BLK
TRI = NB * (NB + 1) // 2
PART = TRI * BLK // 8
HALF = PART // 2

momentum_decay = 0.95
norm_epsilon = 1e-07
first_coef = 3.4445
second_coef = -4.775
third_coef = 2.0315
out_scale = 0.2 * math.sqrt(max(ROWS, C))

f32 = jnp.float32
bf16 = jnp.bfloat16
ALL = ("grp", "row")


def coords(n):
    core = n % 2
    x = (n // 2) % 4
    z_lo = (n // 8) % 2
    y = (n // 16) % 4
    z_hi = n // 64
    return (x, y, z_hi * 2 + z_lo, core)


def number(x, y, z, core):
    return ((((z // 2) * 4 + y) * 2 + z % 2) * 4 + x) * 2 + core


def pairs(move):
    out = []
    for n in range(256):
        x, y, z, core = coords(n)
        out.append((n, number(*move(x, y, z, core))))
    return out


ROUTES = (
    ((2, 2), (1, 2)),
    ((2, 1), (2, 3)),
    ((1, 1), (3, 2)),
    ((1, 3), (3, 1)),
    ((0, 2), (2, 0)),
    ((1, 0), (3, 0)),
    ((0, 1), (0, 3)),
    ((0, 0), (3, 3)),
)
MESSAGE_COUNT = len(ROUTES)


def route(i, sign):
    def move(x, y, z, c):
        dx, dy = ROUTES[i][c]
        return ((x + sign * dx) % 4, (y + sign * dy) % 4, z, c)

    return pairs(move)


def route_codes():
    codes = [0] * GROUPS
    for i, both in enumerate(ROUTES):
        for c, (dx, dy) in enumerate(both):
            codes[dy * 4 + dx] = c * MESSAGE_COUNT + i
    return jnp.array(codes, jnp.int32)


def permute(value, perm):
    return lax.ppermute(value, ALL, perm)


def swap_cores(value):
    return permute(value, pairs(lambda x, y, z, c: (x, y, z, 1 - c)))


def along_z(value, step):
    return permute(value, pairs(lambda x, y, z, c: (x, y, (z + step * (1 - 2 * c)) % 8, c)))


def fill_chosen(table_ref, place_ref, codes_ref, chosen_ref):
    x, y, core = place_ref[0], place_ref[1], place_ref[3]
    for k in range(MATS):
        owner = table_ref[k]

        @pl.when(owner < GROUPS)
        def _():
            code = codes_ref[((((owner >> 2) - y) & 3) << 2) + (((owner & 3) - x) & 3)]
            chosen_ref[code ^ (core * MESSAGE_COUNT)] = k


def nesterov_pieces(first, chosen_ref, grads_ref, mom_ref, outs, gbuf, mbuf, sems):
    def copies(i):
        k = chosen_ref[first + i]
        return (
            pltpu.make_async_copy(grads_ref.at[k], gbuf.at[i], sems.at[0, i]),
            pltpu.make_async_copy(mom_ref.at[k], mbuf.at[i], sems.at[1, i]),
        )

    for i in range(MESSAGE_COUNT):
        for copy in copies(i):
            copy.start()
    for i in range(MESSAGE_COUNT):
        for copy in copies(i):
            copy.wait()
        g = gbuf[i]
        new = momentum_decay * mbuf[i] + g
        outs[i][...] = g + momentum_decay * new


def give_kernel(table_ref, place_ref, codes_ref, grads_ref, mom_ref, chosen_ref, out_a, out_b, gbuf, mbuf, sems):
    fill_chosen(table_ref, place_ref, codes_ref, chosen_ref)
    outs = [out_a.at[pl.ds(i * LINES, LINES)] for i in range(GROUP_A)]
    outs += [out_b.at[pl.ds(i * LINES, LINES)] for i in range(MESSAGE_COUNT - GROUP_A)]
    nesterov_pieces(MESSAGE_COUNT, chosen_ref, grads_ref, mom_ref, outs, gbuf, mbuf, sems)


def keep_kernel(chosen_ref, grads_ref, mom_ref, *refs):
    nesterov_pieces(0, chosen_ref, grads_ref, mom_ref, refs[:MESSAGE_COUNT], *refs[MESSAGE_COUNT:])


def momentum_kernel(table_ref, grads_ref, mom_ref, new_ref):
    for k in range(MATS):
        m = mom_ref[k]
        new_ref[k] = jnp.where(table_ref[k] < GROUPS, momentum_decay * m + grads_ref[k], m)


def gather_rows(messages, x_ref):
    for i, message in enumerate(messages):
        for j in range(NB):
            x_ref[i * MSG_ROWS : (i + 1) * MSG_ROWS, j * BLK : (j + 1) * BLK] = message[pl.ds(j, MSG_ROWS, stride=NB), :]


def split(value):
    hi = value.astype(bf16)
    return hi, (value - hi.astype(f32)).astype(bf16)


def dot(left, right):
    return jnp.dot(left, right, preferred_element_type=f32)


def block_index(i, j):
    return i * NB - i * (i - 1) // 2 + (j - i)


def rows(start, size):
    return pl.ds(pl.multiple_of(start, 8), size)


def gram_kernel(place_ref, *refs):
    messages, keeps, gives = refs[:8], refs[8:12], refs[12:16]
    x_ref, hi_ref, lo_ref, hit_ref, lot_ref, gram_ref = refs[16:]
    gather_rows(messages, x_ref)
    hi, lo = split(x_ref[...])
    hi_ref[...] = hi
    lo_ref[...] = lo
    hit_ref[...] = hi_ref[...].T
    lot_ref[...] = lo_ref[...].T
    for p in range(NT):
        r = slice(p * TILE, (p + 1) * TILE)
        w = slice(p * TILE, C)
        acc = dot(hit_ref[r, :], hi_ref[:, w])
        acc = acc + dot(hit_ref[r, :], lo_ref[:, w])
        acc = acc + dot(lot_ref[r, :], hi_ref[:, w])
        for i in (2 * p, 2 * p + 1):
            for j in range(i, NB):
                b = block_index(i, j)
                gram_ref[b * BLK : (b + 1) * BLK, :] = acc[
                    (i - 2 * p) * BLK : (i - 2 * p + 1) * BLK, (j - 2 * p) * BLK : (j - 2 * p + 1) * BLK
                ]
    z, core = place_ref[2], place_ref[3]
    for outs, c in ((keeps, core), (gives, 1 - core)):
        way = 1 - 2 * c
        for i in (1, 2, 3):
            d = (z + way * i) & 7
            outs[i - 1][:HALF, :] = gram_ref[rows(d * PART + c * HALF, HALF), :]
            outs[i - 1][HALF:, :] = gram_ref[rows(d * PART + (1 - c) * HALF, HALF), :]
        d = (z + 4) & 7
        outs[3][:HALF, :] = gram_ref[rows(d * PART + c * HALF, HALF), :]
        outs[3][HALF:, :] = gram_ref[rows(z * PART + c * HALF, HALF), :]


def diagonal(width):
    row = lax.broadcasted_iota(jnp.int32, (TILE, width), 0)
    col = lax.broadcasted_iota(jnp.int32, (TILE, width), 1)
    return row == col


def tile(p):
    return slice(p * TILE, (p + 1) * TILE)


def put(p, value, out):
    hi, lo = split(value)
    out[0][tile(p), p * TILE :] = hi
    out[1][tile(p), p * TILE :] = lo
    for q in range(p + 1, NT):
        out[0][tile(q), tile(p)] = hi[:, tile(q - p)].T
        out[1][tile(q), tile(p)] = lo[:, tile(q - p)].T


def product(r, w, left, right):
    acc = dot(left[0][r, :], right[0][:, w])
    acc = acc + dot(left[0][r, :], right[1][:, w])
    return acc + dot(left[1][r, :], right[0][:, w])


def polynomial(s, out):
    for p in range(NT):
        r, w = tile(p), slice(p * TILE, C)
        acc = third_coef * product(r, w, s, s)
        acc = acc + second_coef * (s[0][r, w].astype(f32) + s[1][r, w].astype(f32))
        put(p, acc + jnp.where(diagonal(C - p * TILE), first_coef, 0.0), out)


def symmetric_product(left, right, out):
    for p in range(NT):
        put(p, product(tile(p), slice(p * TILE, C), left, right), out)


def step_kernel(place_ref, *refs):
    halves, messages, outs = refs[:16], refs[16:24], refs[24:32]
    gram_ref, x_ref, y_ref, ah, al, bh, bl, ch, cl, xh, xl = refs[32:]
    z, core = place_ref[2], place_ref[3]
    gram_ref[rows(z * PART + core * HALF, HALF), :] = halves[0][...]
    gram_ref[rows(z * PART + (1 - core) * HALF, HALF), :] = halves[1][...]
    for c, parts in ((core, halves[2:9]), (1 - core, halves[9:])):
        way = 1 - 2 * c
        for i, part in enumerate(parts):
            distance, half = (i + 1, c) if i < 4 else (i - 3, 1 - c)
            d = (z - way * distance) & 7
            gram_ref[rows(d * PART + half * HALF, HALF), :] = part[...]
    row = lax.broadcasted_iota(jnp.int32, (BLK, BLK), 0)
    col = lax.broadcasted_iota(jnp.int32, (BLK, BLK), 1)
    diag = jnp.zeros((BLK, BLK), f32)
    for i in range(NB):
        b = block_index(i, i)
        diag = diag + gram_ref[b * BLK : (b + 1) * BLK, :]
    diag = jnp.where(row == col, diag, 0.0)
    total = jnp.sum(jnp.sum(diag, axis=0, keepdims=True), axis=1, keepdims=True)
    inverse = 1.0 / (jnp.sqrt(total) + norm_epsilon)
    for i in range(NB):
        for j in range(i, NB):
            b = block_index(i, j)
            block = gram_ref[b * BLK : (b + 1) * BLK, :] * inverse * inverse
            ri = slice(i * BLK, (i + 1) * BLK)
            rj = slice(j * BLK, (j + 1) * BLK)
            hi, lo = split(block)
            ah[ri, rj], al[ri, rj] = hi, lo
            if j > i:
                ah[rj, ri], al[rj, ri] = hi.T, lo.T
    gather_rows(messages, x_ref)
    hi, lo = split(x_ref[...])
    xh[...] = hi
    xl[...] = lo
    polynomial((ah, al), (bh, bl))
    everything = slice(0, 8 * MSG_ROWS)
    columns = [tile(q) for q in range(NT)]
    for w in columns:
        y_ref[:, w] = product(everything, w, (xh, xl), (bh, bl))
    symmetric_product((ah, al), (bh, bl), (ch, cl))
    symmetric_product((ch, cl), (bh, bl), (ah, al))
    hi, lo = split(y_ref[...])
    xh[...] = hi
    xl[...] = lo
    for w in columns:
        x_ref[:, w] = third_coef * product(everything, w, (xh, xl), (ah, al)) + second_coef * y_ref[:, w]
    hi, lo = split(x_ref[...])
    xh[...] = hi
    xl[...] = lo
    factor = inverse * out_scale
    for q, w in enumerate(columns):
        result = (product(everything, w, (xh, xl), (ah, al)) + first_coef * y_ref[:, w]) * factor
        for i, out_ref in enumerate(outs):
            for j in range(TILE // BLK):
                out_ref[pl.ds(q * (TILE // BLK) + j, MSG_ROWS, stride=NB), :] = result[
                    i * MSG_ROWS : (i + 1) * MSG_ROWS, j * BLK : (j + 1) * BLK
                ]


def piece_copies(first, chosen_ref, pieces, update_ref, sems):
    return [
        pltpu.make_async_copy(piece, update_ref.at[chosen_ref[first + i]], sems.at[i]) for i, piece in enumerate(pieces)
    ]


def own_update_kernel(table_ref, chosen_ref, *refs):
    messages, (update_ref, zero_ref, sems) = refs[:MESSAGE_COUNT], refs[MESSAGE_COUNT:]
    zero_ref[...] = jnp.zeros((LINES, BLK), f32)
    pieces = [message.at[pl.ds(0, LINES)] for message in messages]

    def zero_copy(k):
        return pltpu.make_async_copy(zero_ref, update_ref.at[k], sems.at[MESSAGE_COUNT + k])

    for copy in piece_copies(0, chosen_ref, pieces, update_ref, sems):
        copy.start()
    for k in range(MATS):
        pl.when(table_ref[k] >= GROUPS)(lambda k=k: zero_copy(k).start())
    for copy in piece_copies(0, chosen_ref, pieces, update_ref, sems):
        copy.wait()
    for k in range(MATS):
        pl.when(table_ref[k] >= GROUPS)(lambda k=k: zero_copy(k).wait())


def other_update_kernel(chosen_ref, in_a, in_b, _, update_ref, sems):
    pieces = [in_a.at[pl.ds(i * LINES, LINES)] for i in range(MESSAGE_COUNT - GROUP_B)]
    pieces += [in_b.at[pl.ds(i * LINES, LINES)] for i in range(GROUP_B)]
    for copy in piece_copies(MESSAGE_COUNT, chosen_ref, pieces, update_ref, sems):
        copy.start()
    for copy in piece_copies(MESSAGE_COUNT, chosen_ref, pieces, update_ref, sems):
        copy.wait()


VMEM = pl.BlockSpec(memory_space=pltpu.VMEM)
SMEM = pl.BlockSpec(memory_space=pltpu.SMEM)
HBM = pl.BlockSpec(memory_space=pltpu.HBM)


def shape(*dims):
    return jax.ShapeDtypeStruct(dims, f32)


def call(kernel, in_specs, out_shape, scratch, name, flops, moved, mib, out_specs=None, aliases={}):
    return pl.pallas_call(
        kernel,
        in_specs=in_specs,
        out_specs=out_specs or jax.tree.map(lambda _: VMEM, out_shape),
        input_output_aliases=aliases,
        out_shape=out_shape,
        scratch_shapes=scratch,
        name=name,
        cost_estimate=pl.CostEstimate(flops=flops, bytes_accessed=moved, transcendentals=0),
        compiler_params=pltpu.CompilerParams(vmem_limit_bytes=mib * 1024 * 1024),
    )


MESSAGES = [shape(MSG_LINES, BLK)] * MESSAGE_COUNT
MSG_BYTES = MESSAGE_COUNT * MSG_LINES * BLK * 4


def shards(grads, momentum, owner_table):
    grp, row = lax.axis_index("grp"), lax.axis_index("row")
    core = row % 2
    place = jnp.stack([(row // 2) % 4, grp % 4, (grp // 4) * 2 + row // 8, core]).astype(jnp.int32)
    lines = (MATS, LINES, BLK)
    grads, momentum = grads.reshape(lines), momentum.reshape(lines)

    buffers = [pltpu.VMEM((MESSAGE_COUNT, LINES, BLK), f32)] * 2 + [pltpu.SemaphoreType.DMA((2, MESSAGE_COUNT))]
    chosen, give_a, give_b = call(
        give_kernel, [SMEM, SMEM, SMEM, HBM, HBM],
        [
            jax.ShapeDtypeStruct((GROUPS,), jnp.int32),
            shape(GROUP_A * LINES, BLK),
            shape((MESSAGE_COUNT - GROUP_A) * LINES, BLK),
        ],
        buffers, "give", 0, 3 * MSG_BYTES // 2, 53, [SMEM, VMEM, VMEM],
    )(owner_table, place, route_codes(), grads, momentum)
    keep = call(
        keep_kernel, [SMEM, HBM, HBM], [shape(LINES, BLK)] * MESSAGE_COUNT, buffers, "keep", 0, 3 * MSG_BYTES // 2, 50,
    )(chosen, grads, momentum)
    taken = [swap_cores(give_a), swap_cores(give_b)]
    owned = []
    for i in range(MESSAGE_COUNT):
        part, at = (taken[0], i) if i < GROUP_A else (taken[1], i - GROUP_A)
        message = jnp.concatenate([keep[i], part[at * LINES : (at + 1) * LINES]])
        owned.append(permute(message, route(i, 1)))

    tall = [pltpu.VMEM((8 * MSG_ROWS, C), bf16)] * 2
    whole = pltpu.VMEM((8 * MSG_ROWS, C), f32)
    triangle = pltpu.VMEM((TRI * BLK, BLK), f32)
    sums = call(
        gram_kernel, [SMEM] + [VMEM] * 8, [shape(PART, BLK)] * 8,
        [whole] + tall + [pltpu.VMEM((C, 8 * MSG_ROWS), bf16)] * 2 + [triangle],
        "gram", 3 * 8 * MSG_ROWS * C * C, MSG_BYTES + 8 * PART * BLK * 4, 20,
    )(place, *owned)
    keeps, gives = sums[:4], sums[4:]

    distant = keeps[2] + swap_cores(gives[2])
    ends = keeps[3] + swap_cores(gives[3])
    distant, ends, late_near, late_middle = lax.optimization_barrier((distant, ends, gives[0], gives[1]))
    near = keeps[0] + swap_cores(late_near)
    middle = keeps[1] + swap_cores(late_middle)
    moved = [middle[:HALF] + along_z(ends[:HALF], 2) + along_z(distant[:HALF], 1)]
    moved.append(middle[HALF:] + along_z(distant[HALF:], 1))
    moved = [along_z(moved[h], 2) + along_z(near[h * HALF : (h + 1) * HALF], 1) for h in range(2)]
    moved[0] = moved[0] + ends[HALF:]
    own = [moved[0] + swap_cores(moved[1]), moved[1] + swap_cores(moved[0])]

    second = [along_z(half, 2) for half in own]
    first = [along_z(half, 1) for half in own]

    late_table, _ = lax.optimization_barrier((owner_table, own[0]))
    new_momentum = call(
        momentum_kernel, [SMEM, VMEM, VMEM], shape(*lines), [], "momentum", 0, 6 * MSG_BYTES, 12,
    )(late_table, grads, momentum)
    new_momentum, second[1] = lax.optimization_barrier((new_momentum, second[1]))

    third = [along_z(half, 1) for half in second]
    fourth = along_z(second[0], 2)
    gathered = [first[0], second[0], third[0], fourth, first[1], second[1], third[1]]
    halves = own + gathered + [swap_cores(half) for half in gathered]

    results = call(
        step_kernel, [SMEM] + [VMEM] * 24, MESSAGES,
        [triangle, whole, whole] + [pltpu.VMEM((C, C), bf16)] * 6 + tall,
        "newton", 6 * (3 * C * C * C * 5 // 8 + 3 * 8 * MSG_ROWS * C * C), 2 * MSG_BYTES + 4 * TRI * BLK * BLK, 36,
    )(place, *halves, *owned)

    back = [permute(result, route(i, -1)) for i, result in enumerate(results)]
    update = call(
        own_update_kernel, [SMEM, SMEM] + [VMEM] * MESSAGE_COUNT, shape(*lines),
        [pltpu.VMEM((LINES, BLK), f32), pltpu.SemaphoreType.DMA((MESSAGE_COUNT + MATS,))],
        "own_update", 0, MSG_BYTES, 4, HBM,
    )(owner_table, chosen, *back)
    others = [message[LINES:] for message in back]
    others = [jnp.concatenate(others[:-GROUP_B]), jnp.concatenate(others[-GROUP_B:])]
    update = call(
        other_update_kernel, [SMEM, VMEM, VMEM, HBM], shape(*lines), [pltpu.SemaphoreType.DMA((MESSAGE_COUNT,))],
        "other_update", 0, MSG_BYTES, 4, HBM, {3: 0},
    )(chosen, *[swap_cores(part) for part in others], update)
    state = (MATS, 1, LINES * BLK // C, C)
    return (new_momentum.reshape(state), update.reshape(state))


def solution(mesh):
    in_specs = (P(None, "row", "grp", None), P(None, "row", "grp", None), P())
    out_specs = (P(None, "row", "grp", None), P(None, "row", "grp", None))
    return jax.shard_map(shards, mesh=mesh, in_specs=in_specs, out_specs=out_specs, check_vma=False)
```

```python
import functools
import math

import jax
import jax.numpy as jnp
from jax import lax
from jax.experimental import pallas as pl
from jax.experimental.pallas import tpu as pltpu
from jax.sharding import PartitionSpec as P

MATS = 24
GROUPS = 16
C = 1024
PIECE_ROWS = 14
LINES = PIECE_ROWS * C // 128
MSG_ROWS = 4 * PIECE_ROWS
MSG_LINES = 4 * LINES
BAND = 2 * MSG_ROWS
ROWS = 7168
TILE = 256
NT = C // TILE
BLK = 128
NB = C // BLK
TRI = NB * (NB + 1) // 2
PART = TRI * BLK // 8
HALF = PART // 2

momentum_decay = 0.95
norm_epsilon = 1e-07
first_coef = 3.4445
second_coef = -4.775
third_coef = 2.0315
out_scale = 0.2 * math.sqrt(max(ROWS, C))

f32 = jnp.float32
bf16 = jnp.bfloat16
ALL = ("grp", "row")


def coords(n):
    core = n % 2
    x = (n // 2) % 4
    z_lo = (n // 8) % 2
    y = (n // 16) % 4
    z_hi = n // 64
    return (x, y, z_hi * 2 + z_lo, core)


def number(x, y, z, core):
    return ((((z // 2) * 4 + y) * 2 + z % 2) * 4 + x) * 2 + core


def pairs(move):
    out = []
    for n in range(256):
        x, y, z, core = coords(n)
        out.append((n, number(*move(x, y, z, core))))
    return out


def first_axis(step):
    return pairs(
        lambda x, y, z, c: ((x + step) % 4, y, z, c) if c == 0 else (x, (y + step) % 4, z, c)
    )


def second_axis(step):
    return pairs(
        lambda x, y, z, c: (x, (y + step) % 4, z, c) if c == 0 else ((x + step) % 4, y, z, c)
    )


def permute(value, perm):
    return lax.ppermute(value, ALL, perm)


def swap_cores(value):
    return permute(value, pairs(lambda x, y, z, c: (x, y, z, 1 - c)))


def along_z(value, step):
    return permute(value, pairs(lambda x, y, z, c: (x, y, (z + step * (1 - 2 * c)) % 8, c)))


def fill_chosen(table_ref, place_ref, chosen_ref):
    x, y, core = place_ref[0], place_ref[1], place_ref[3]
    for k in range(MATS):
        owner = table_ref[k]

        @pl.when(owner < GROUPS)
        def _():
            dx = ((owner & 3) - x) & 3
            dy = ((owner >> 2) - y) & 3
            slot = jnp.where(core == 0, dx * 4 + dy, dy * 4 + dx)
            chosen_ref[slot] = k


def half_slot(half, slot):
    return slot % 4 * 4 + slot // 4 if half else slot


def outgoing_kernel(half, table_ref, place_ref, grads_ref, mom_ref, chosen_ref, o0, o1, o2, o3, gbuf, mbuf, sems):
    lines = pl.ds(half * LINES, LINES)
    grads_copy = pltpu.make_async_copy(grads_ref.at[:, lines], gbuf, sems.at[0])
    mom_copy = pltpu.make_async_copy(mom_ref.at[:, lines], mbuf, sems.at[1])
    grads_copy.start()
    mom_copy.start()
    if half == 0:
        fill_chosen(table_ref, place_ref, chosen_ref)
    grads_copy.wait()
    mom_copy.wait()
    outs = (o0, o1, o2, o3)
    for slot in range(GROUPS):
        k = chosen_ref[half_slot(half, slot)]
        g = gbuf[k]
        new = momentum_decay * mbuf[k] + g
        t = slot % 4
        outs[slot // 4][t * LINES : (t + 1) * LINES, :] = g + momentum_decay * new


def momentum_kernel(table_ref, grads_ref, mom_ref, new_ref):
    for k in range(MATS):
        m = mom_ref[k]
        new_ref[k] = jnp.where(table_ref[k] < GROUPS, momentum_decay * m + grads_ref[k], m)


def regroup_kernel(i0, i1, i2, i3, o0, o1, o2, o3):
    ins, outs = (i0, i1, i2, i3), (o0, o1, o2, o3)
    for t in range(4):
        for s in range(4):
            outs[t][s * LINES : (s + 1) * LINES, :] = ins[s][t * LINES : (t + 1) * LINES, :]


def gather_rows(messages, x_ref):
    for h in range(2):
        for t in range(4):
            at = slice((h * 4 + t) * MSG_ROWS, (h * 4 + t + 1) * MSG_ROWS)
            for j in range(NB):
                x_ref[at, j * BLK : (j + 1) * BLK] = messages[4 * h + t][pl.ds(j, MSG_ROWS, stride=NB), :]


def split(value):
    hi = value.astype(bf16)
    return hi, (value - hi.astype(f32)).astype(bf16)


def dot(left, right):
    return jnp.dot(left, right, preferred_element_type=f32)


def block_index(i, j):
    return i * NB - i * (i - 1) // 2 + (j - i)


def rows(start, size):
    return pl.ds(pl.multiple_of(start, 8), size)


def gram_kernel(place_ref, *refs):
    messages, keeps, gives = refs[:8], refs[8:12], refs[12:16]
    x_ref, hi_ref, lo_ref, hit_ref, lot_ref, gram_ref = refs[16:]
    gather_rows(messages, x_ref)
    hi, lo = split(x_ref[...])
    hi_ref[...] = hi
    lo_ref[...] = lo
    hit_ref[...] = hi_ref[...].T
    lot_ref[...] = lo_ref[...].T
    for p in range(NT):
        r = slice(p * TILE, (p + 1) * TILE)
        w = slice(p * TILE, C)
        acc = dot(hit_ref[r, :], hi_ref[:, w])
        acc = acc + dot(hit_ref[r, :], lo_ref[:, w])
        acc = acc + dot(lot_ref[r, :], hi_ref[:, w])
        for i in (2 * p, 2 * p + 1):
            for j in range(i, NB):
                b = block_index(i, j)
                gram_ref[b * BLK : (b + 1) * BLK, :] = acc[
                    (i - 2 * p) * BLK : (i - 2 * p + 1) * BLK, (j - 2 * p) * BLK : (j - 2 * p + 1) * BLK
                ]
    z, core = place_ref[2], place_ref[3]
    for outs, c in ((keeps, core), (gives, 1 - core)):
        way = 1 - 2 * c
        for i in (1, 2, 3):
            d = (z + way * i) & 7
            outs[i - 1][:HALF, :] = gram_ref[rows(d * PART + c * HALF, HALF), :]
            outs[i - 1][HALF:, :] = gram_ref[rows(d * PART + (1 - c) * HALF, HALF), :]
        d = (z + 4) & 7
        outs[3][:HALF, :] = gram_ref[rows(d * PART + c * HALF, HALF), :]
        outs[3][HALF:, :] = gram_ref[rows(z * PART + c * HALF, HALF), :]


def diagonal(width):
    row = lax.broadcasted_iota(jnp.int32, (TILE, width), 0)
    col = lax.broadcasted_iota(jnp.int32, (TILE, width), 1)
    return row == col


def tile(p):
    return slice(p * TILE, (p + 1) * TILE)


def put(p, value, out):
    hi, lo = split(value)
    out[0][tile(p), p * TILE :] = hi
    out[1][tile(p), p * TILE :] = lo
    for q in range(p + 1, NT):
        out[0][tile(q), tile(p)] = hi[:, tile(q - p)].T
        out[1][tile(q), tile(p)] = lo[:, tile(q - p)].T


def product(r, w, left, right):
    acc = dot(left[0][r, :], right[0][:, w])
    acc = acc + dot(left[0][r, :], right[1][:, w])
    return acc + dot(left[1][r, :], right[0][:, w])


def polynomial(s, out):
    for p in range(NT):
        r, w = tile(p), slice(p * TILE, C)
        acc = third_coef * product(r, w, s, s)
        acc = acc + second_coef * (s[0][r, w].astype(f32) + s[1][r, w].astype(f32))
        put(p, acc + jnp.where(diagonal(C - p * TILE), first_coef, 0.0), out)


def symmetric_product(left, right, out):
    for p in range(NT):
        put(p, product(tile(p), slice(p * TILE, C), left, right), out)


def step_kernel(place_ref, *refs):
    halves, messages, outs = refs[:16], refs[16:24], refs[24:32]
    gram_ref, x_ref, y_ref, ah, al, bh, bl, ch, cl, xh, xl = refs[32:]
    z, core = place_ref[2], place_ref[3]
    gram_ref[rows(z * PART + core * HALF, HALF), :] = halves[0][...]
    gram_ref[rows(z * PART + (1 - core) * HALF, HALF), :] = halves[1][...]
    for c, parts in ((core, halves[2:9]), (1 - core, halves[9:])):
        way = 1 - 2 * c
        for i, part in enumerate(parts):
            distance, half = (i + 1, c) if i < 4 else (i - 3, 1 - c)
            d = (z - way * distance) & 7
            gram_ref[rows(d * PART + half * HALF, HALF), :] = part[...]
    row = lax.broadcasted_iota(jnp.int32, (BLK, BLK), 0)
    col = lax.broadcasted_iota(jnp.int32, (BLK, BLK), 1)
    diag = jnp.zeros((BLK, BLK), f32)
    for i in range(NB):
        b = block_index(i, i)
        diag = diag + gram_ref[b * BLK : (b + 1) * BLK, :]
    diag = jnp.where(row == col, diag, 0.0)
    total = jnp.sum(jnp.sum(diag, axis=0, keepdims=True), axis=1, keepdims=True)
    inverse = 1.0 / (jnp.sqrt(total) + norm_epsilon)
    for i in range(NB):
        for j in range(i, NB):
            b = block_index(i, j)
            block = gram_ref[b * BLK : (b + 1) * BLK, :] * inverse * inverse
            ri = slice(i * BLK, (i + 1) * BLK)
            rj = slice(j * BLK, (j + 1) * BLK)
            hi, lo = split(block)
            ah[ri, rj], al[ri, rj] = hi, lo
            if j > i:
                ah[rj, ri], al[rj, ri] = hi.T, lo.T
    gather_rows(messages, x_ref)
    hi, lo = split(x_ref[...])
    xh[...] = hi
    xl[...] = lo
    polynomial((ah, al), (bh, bl))
    everything = slice(0, 8 * MSG_ROWS)
    columns = [tile(q) for q in range(NT)]
    for w in columns:
        y_ref[:, w] = product(everything, w, (xh, xl), (bh, bl))
    symmetric_product((ah, al), (bh, bl), (ch, cl))
    symmetric_product((ch, cl), (bh, bl), (ah, al))
    hi, lo = split(y_ref[...])
    xh[...] = hi
    xl[...] = lo
    for w in columns:
        x_ref[:, w] = third_coef * product(everything, w, (xh, xl), (ah, al)) + second_coef * y_ref[:, w]
    hi, lo = split(x_ref[...])
    xh[...] = hi
    xl[...] = lo
    factor = inverse * out_scale
    for q, w in enumerate(columns):
        result = (product(everything, w, (xh, xl), (ah, al)) + first_coef * y_ref[:, w]) * factor
        for i, out_ref in enumerate(outs):
            for j in range(TILE // BLK):
                out_ref[pl.ds(q * (TILE // BLK) + j, MSG_ROWS, stride=NB), :] = result[
                    i * MSG_ROWS : (i + 1) * MSG_ROWS, j * BLK : (j + 1) * BLK
                ]


def update_kernel(half, table_ref, chosen_ref, i0, i1, i2, i3, *refs):
    update_ref, zero_ref, sems = refs[-3:]
    lines = pl.ds(half * LINES, LINES)
    zero_ref[...] = jnp.zeros((LINES, BLK), f32)

    def piece_copy(slot):
        source = (i0, i1, i2, i3)[slot // 4].at[pl.ds(slot % 4 * LINES, LINES)]
        return pltpu.make_async_copy(source, update_ref.at[chosen_ref[half_slot(half, slot)], lines], sems.at[slot])

    def zero_copy(k):
        return pltpu.make_async_copy(zero_ref, update_ref.at[k, lines], sems.at[GROUPS + k])

    for slot in range(GROUPS):
        piece_copy(slot).start()
    for k in range(MATS):
        pl.when(table_ref[k] >= GROUPS)(lambda k=k: zero_copy(k).start())
    for slot in range(GROUPS):
        piece_copy(slot).wait()
    for k in range(MATS):
        pl.when(table_ref[k] >= GROUPS)(lambda k=k: zero_copy(k).wait())


VMEM = pl.BlockSpec(memory_space=pltpu.VMEM)
SMEM = pl.BlockSpec(memory_space=pltpu.SMEM)
HBM = pl.BlockSpec(memory_space=pltpu.HBM)


def shape(*dims):
    return jax.ShapeDtypeStruct(dims, f32)


def call(kernel, in_specs, out_shape, scratch, name, flops, moved, mib, out_specs=None, aliases={}):
    return pl.pallas_call(
        kernel,
        in_specs=in_specs,
        out_specs=out_specs or jax.tree.map(lambda _: VMEM, out_shape),
        input_output_aliases=aliases,
        out_shape=out_shape,
        scratch_shapes=scratch,
        name=name,
        cost_estimate=pl.CostEstimate(flops=flops, bytes_accessed=moved, transcendentals=0),
        compiler_params=pltpu.CompilerParams(vmem_limit_bytes=mib * 1024 * 1024),
    )


MESSAGES = [shape(MSG_LINES, BLK)] * 4
MSG_BYTES = 8 * MSG_LINES * BLK * 4


def exchange(messages, regroup, half, outward):
    first, second = (first_axis, second_axis) if outward == (half == 0) else (second_axis, first_axis)
    sign = 1 if outward else -1
    middle = [messages[0]] + [permute(messages[s], first(sign * s)) for s in (1, 2, 3)]
    middle = regroup(*middle)
    return [middle[0]] + [permute(middle[t], second(sign * t)) for t in (1, 2, 3)]


def shards(grads, momentum, owner_table):
    grp, row = lax.axis_index("grp"), lax.axis_index("row")
    core = row % 2
    place = jnp.stack([(row // 2) % 4, grp % 4, (grp // 4) * 2 + row // 8, core]).astype(jnp.int32)
    lines = (MATS, 2 * LINES, BLK)
    grads, momentum = grads.reshape(lines), momentum.reshape(lines)

    buffers = [pltpu.VMEM((MATS, LINES, BLK), f32)] * 2 + [pltpu.SemaphoreType.DMA((2,))]
    chosen, *first_rows = call(
        functools.partial(outgoing_kernel, 0), [SMEM, SMEM, HBM, HBM],
        [jax.ShapeDtypeStruct((GROUPS,), jnp.int32)] + MESSAGES, buffers,
        "outgoing", 0, 2 * MSG_BYTES, 48, [SMEM] + [VMEM] * 4,
    )(owner_table, place, grads, momentum)
    last_rows = call(
        functools.partial(outgoing_kernel, 1), [SMEM, SMEM, HBM, HBM, SMEM], MESSAGES, buffers,
        "outgoing", 0, 2 * MSG_BYTES, 48,
    )(owner_table, place, grads, momentum, chosen)

    regroup = call(regroup_kernel, [VMEM] * 4, MESSAGES, [], "regroup", 0, MSG_BYTES, 4)
    owned = exchange(first_rows, regroup, 0, True) + exchange(last_rows, regroup, 1, True)

    tall = [pltpu.VMEM((8 * MSG_ROWS, C), bf16)] * 2
    whole = pltpu.VMEM((8 * MSG_ROWS, C), f32)
    triangle = pltpu.VMEM((TRI * BLK, BLK), f32)
    sums = call(
        gram_kernel, [SMEM] + [VMEM] * 8, [shape(PART, BLK)] * 8,
        [whole] + tall + [pltpu.VMEM((C, 8 * MSG_ROWS), bf16)] * 2 + [triangle],
        "gram", 3 * 8 * MSG_ROWS * C * C, MSG_BYTES + 8 * PART * BLK * 4, 20,
    )(place, *owned)
    keeps, gives = sums[:4], sums[4:]

    distant = keeps[2] + swap_cores(gives[2])
    ends = keeps[3] + swap_cores(gives[3])
    distant, ends, late_near, late_middle = lax.optimization_barrier((distant, ends, gives[0], gives[1]))
    near = keeps[0] + swap_cores(late_near)
    middle = keeps[1] + swap_cores(late_middle)
    moved = [middle[:HALF] + along_z(ends[:HALF], 2) + along_z(distant[:HALF], 1)]
    moved.append(middle[HALF:] + along_z(distant[HALF:], 1))
    moved = [along_z(moved[h], 2) + along_z(near[h * HALF : (h + 1) * HALF], 1) for h in range(2)]
    moved[0] = moved[0] + ends[HALF:]
    own = [moved[0] + swap_cores(moved[1]), moved[1] + swap_cores(moved[0])]

    second = [along_z(half, 2) for half in own]
    first = [along_z(half, 1) for half in own]

    late_table, _ = lax.optimization_barrier((owner_table, own[0]))
    new_momentum = call(
        momentum_kernel, [SMEM, VMEM, VMEM], shape(*lines), [], "momentum", 0, 6 * MSG_BYTES, 12,
    )(late_table, grads, momentum)
    new_momentum, second[1] = lax.optimization_barrier((new_momentum, second[1]))

    third = [along_z(half, 1) for half in second]
    fourth = along_z(second[0], 2)
    gathered = [first[0], second[0], third[0], fourth, first[1], second[1], third[1]]
    halves = own + gathered + [swap_cores(half) for half in gathered]

    results = call(
        step_kernel, [SMEM] + [VMEM] * 24, MESSAGES * 2,
        [triangle, whole, whole] + [pltpu.VMEM((C, C), bf16)] * 6 + tall,
        "newton", 6 * (3 * C * C * C * 5 // 8 + 3 * 8 * MSG_ROWS * C * C), 2 * MSG_BYTES + 4 * TRI * BLK * BLK, 36,
    )(place, *halves, *owned)

    update = []
    for half in range(2):
        back = exchange(results[4 * half : 4 * half + 4], regroup, half, False)
        update = [
            call(
                functools.partial(update_kernel, half), [SMEM, SMEM] + [VMEM] * 4 + [HBM] * half, shape(*lines),
                [pltpu.VMEM((LINES, BLK), f32), pltpu.SemaphoreType.DMA((GROUPS + MATS,))],
                "update", 0, MSG_BYTES, 4, HBM, {6: 0} if half else {},
            )(owner_table, chosen, *back, *update)
        ]
    update = update[0]
    state = (MATS, 1, 2 * LINES * BLK // C, C)
    return (new_momentum.reshape(state), update.reshape(state))


def solution(mesh):
    in_specs = (P(None, "row", "grp", None), P(None, "row", "grp", None), P())
    out_specs = (P(None, "row", "grp", None), P(None, "row", "grp", None))
    return jax.shard_map(shards, mesh=mesh, in_specs=in_specs, out_specs=out_specs, check_vma=False)
```

```python
import functools
import math

import jax
import jax.numpy as jnp
from jax import lax
from jax.experimental import pallas as pl
from jax.experimental.pallas import tpu as pltpu
from jax.sharding import PartitionSpec as P

MATS = 24
GROUPS = 16
C = 1024
PIECE_ROWS = 14
LINES = PIECE_ROWS * C // 128
MSG_ROWS = 4 * PIECE_ROWS
MSG_LINES = 4 * LINES
BAND = 2 * MSG_ROWS
ROWS = 7168
TILE = 256
NT = C // TILE
BLK = 128
NB = C // BLK
TRI = NB * (NB + 1) // 2
PART = TRI * BLK // 8
HALF = PART // 2

momentum_decay = 0.95
norm_epsilon = 1e-07
first_coef = 3.4445
second_coef = -4.775
third_coef = 2.0315
out_scale = 0.2 * math.sqrt(max(ROWS, C))

f32 = jnp.float32
bf16 = jnp.bfloat16
ALL = ("grp", "row")


def coords(n):
    core = n % 2
    x = (n // 2) % 4
    z_lo = (n // 8) % 2
    y = (n // 16) % 4
    z_hi = n // 64
    return (x, y, z_hi * 2 + z_lo, core)


def number(x, y, z, core):
    return ((((z // 2) * 4 + y) * 2 + z % 2) * 4 + x) * 2 + core


def pairs(move):
    out = []
    for n in range(256):
        x, y, z, core = coords(n)
        out.append((n, number(*move(x, y, z, core))))
    return out


def first_axis(step):
    return pairs(
        lambda x, y, z, c: ((x + step) % 4, y, z, c) if c == 0 else (x, (y + step) % 4, z, c)
    )


def second_axis(step):
    return pairs(
        lambda x, y, z, c: (x, (y + step) % 4, z, c) if c == 0 else ((x + step) % 4, y, z, c)
    )


def permute(value, perm):
    return lax.ppermute(value, ALL, perm)


def swap_cores(value):
    return permute(value, pairs(lambda x, y, z, c: (x, y, z, 1 - c)))


def along_z(value, step):
    return permute(value, pairs(lambda x, y, z, c: (x, y, (z + step * (1 - 2 * c)) % 8, c)))


def fill_chosen(table_ref, place_ref, chosen_ref):
    x, y, core = place_ref[0], place_ref[1], place_ref[3]
    for k in range(MATS):
        owner = table_ref[k]

        @pl.when(owner < GROUPS)
        def _():
            dx = ((owner & 3) - x) & 3
            dy = ((owner >> 2) - y) & 3
            slot = jnp.where(core == 0, dx * 4 + dy, dy * 4 + dx)
            chosen_ref[slot] = k


def half_slot(half, slot):
    return slot % 4 * 4 + slot // 4 if half else slot


def outgoing_kernel(half, table_ref, place_ref, grads_ref, mom_ref, chosen_ref, o0, o1, o2, o3, gbuf, mbuf, sems):
    lines = pl.ds(half * LINES, LINES)
    grads_copy = pltpu.make_async_copy(grads_ref.at[:, lines], gbuf, sems.at[0])
    mom_copy = pltpu.make_async_copy(mom_ref.at[:, lines], mbuf, sems.at[1])
    grads_copy.start()
    mom_copy.start()
    if half == 0:
        fill_chosen(table_ref, place_ref, chosen_ref)
    grads_copy.wait()
    mom_copy.wait()
    outs = (o0, o1, o2, o3)
    for slot in range(GROUPS):
        k = chosen_ref[half_slot(half, slot)]
        g = gbuf[k]
        new = momentum_decay * mbuf[k] + g
        t = slot % 4
        outs[slot // 4][t * LINES : (t + 1) * LINES, :] = g + momentum_decay * new


def momentum_kernel(table_ref, grads_ref, mom_ref, new_ref):
    for k in range(MATS):
        m = mom_ref[k]
        new_ref[k] = jnp.where(table_ref[k] < GROUPS, momentum_decay * m + grads_ref[k], m)


def regroup_kernel(i0, i1, i2, i3, o0, o1, o2, o3):
    ins, outs = (i0, i1, i2, i3), (o0, o1, o2, o3)
    for t in range(4):
        for s in range(4):
            outs[t][s * LINES : (s + 1) * LINES, :] = ins[s][t * LINES : (t + 1) * LINES, :]


def gather_rows(messages, x_ref):
    for h in range(2):
        for t in range(4):
            at = slice((h * 4 + t) * MSG_ROWS, (h * 4 + t + 1) * MSG_ROWS)
            for j in range(NB):
                x_ref[at, j * BLK : (j + 1) * BLK] = messages[4 * h + t][pl.ds(j, MSG_ROWS, stride=NB), :]


def split(value):
    hi = value.astype(bf16)
    return hi, (value - hi.astype(f32)).astype(bf16)


def dot(left, right):
    return jnp.dot(left, right, preferred_element_type=f32)


def block_index(i, j):
    return i * NB - i * (i - 1) // 2 + (j - i)


def rows(start, size):
    return pl.ds(pl.multiple_of(start, 8), size)


def gram_kernel(place_ref, *refs):
    messages, keeps, gives = refs[:8], refs[8:12], refs[12:16]
    x_ref, hi_ref, lo_ref, hit_ref, lot_ref, gram_ref = refs[16:]
    gather_rows(messages, x_ref)
    hi, lo = split(x_ref[...])
    hi_ref[...] = hi
    lo_ref[...] = lo
    hit_ref[...] = hi_ref[...].T
    lot_ref[...] = lo_ref[...].T
    for p in range(NT):
        r = slice(p * TILE, (p + 1) * TILE)
        w = slice(p * TILE, C)
        acc = dot(hit_ref[r, :], hi_ref[:, w])
        acc = acc + dot(hit_ref[r, :], lo_ref[:, w])
        acc = acc + dot(lot_ref[r, :], hi_ref[:, w])
        for i in (2 * p, 2 * p + 1):
            for j in range(i, NB):
                b = block_index(i, j)
                gram_ref[b * BLK : (b + 1) * BLK, :] = acc[
                    (i - 2 * p) * BLK : (i - 2 * p + 1) * BLK, (j - 2 * p) * BLK : (j - 2 * p + 1) * BLK
                ]
    z, core = place_ref[2], place_ref[3]
    for outs, c in ((keeps, core), (gives, 1 - core)):
        way = 1 - 2 * c
        for i in (1, 2, 3):
            d = (z + way * i) & 7
            outs[i - 1][:HALF, :] = gram_ref[rows(d * PART + c * HALF, HALF), :]
            outs[i - 1][HALF:, :] = gram_ref[rows(d * PART + (1 - c) * HALF, HALF), :]
        d = (z + 4) & 7
        outs[3][:HALF, :] = gram_ref[rows(d * PART + c * HALF, HALF), :]
        outs[3][HALF:, :] = gram_ref[rows(z * PART + c * HALF, HALF), :]


def diagonal(width):
    row = lax.broadcasted_iota(jnp.int32, (TILE, width), 0)
    col = lax.broadcasted_iota(jnp.int32, (TILE, width), 1)
    return row == col


def tile(p):
    return slice(p * TILE, (p + 1) * TILE)


def put(p, value, out):
    hi, lo = split(value)
    out[0][tile(p), p * TILE :] = hi
    out[1][tile(p), p * TILE :] = lo
    for q in range(p + 1, NT):
        out[0][tile(q), tile(p)] = hi[:, tile(q - p)].T
        out[1][tile(q), tile(p)] = lo[:, tile(q - p)].T


def product(r, w, left, right):
    acc = dot(left[0][r, :], right[0][:, w])
    acc = acc + dot(left[0][r, :], right[1][:, w])
    return acc + dot(left[1][r, :], right[0][:, w])


def polynomial(s, out):
    for p in range(NT):
        r, w = tile(p), slice(p * TILE, C)
        acc = third_coef * product(r, w, s, s)
        acc = acc + second_coef * (s[0][r, w].astype(f32) + s[1][r, w].astype(f32))
        put(p, acc + jnp.where(diagonal(C - p * TILE), first_coef, 0.0), out)


def symmetric_product(left, right, out):
    for p in range(NT):
        put(p, product(tile(p), slice(p * TILE, C), left, right), out)


def step_kernel(place_ref, *refs):
    halves, messages = refs[:16], refs[16:24]
    y_ref, xh, xl, ah, al, gram_ref, x_ref, bh, bl, ch, cl = refs[24:]
    z, core = place_ref[2], place_ref[3]
    gram_ref[rows(z * PART + core * HALF, HALF), :] = halves[0][...]
    gram_ref[rows(z * PART + (1 - core) * HALF, HALF), :] = halves[1][...]
    for c, parts in ((core, halves[2:9]), (1 - core, halves[9:])):
        way = 1 - 2 * c
        for i, part in enumerate(parts):
            distance, half = (i + 1, c) if i < 4 else (i - 3, 1 - c)
            d = (z - way * distance) & 7
            gram_ref[rows(d * PART + half * HALF, HALF), :] = part[...]
    row = lax.broadcasted_iota(jnp.int32, (BLK, BLK), 0)
    col = lax.broadcasted_iota(jnp.int32, (BLK, BLK), 1)
    diag = jnp.zeros((BLK, BLK), f32)
    for i in range(NB):
        b = block_index(i, i)
        diag = diag + gram_ref[b * BLK : (b + 1) * BLK, :]
    diag = jnp.where(row == col, diag, 0.0)
    total = jnp.sum(jnp.sum(diag, axis=0, keepdims=True), axis=1, keepdims=True)
    inverse = 1.0 / (jnp.sqrt(total) + norm_epsilon)
    for i in range(NB):
        for j in range(i, NB):
            b = block_index(i, j)
            block = gram_ref[b * BLK : (b + 1) * BLK, :] * inverse * inverse
            ri = slice(i * BLK, (i + 1) * BLK)
            rj = slice(j * BLK, (j + 1) * BLK)
            hi, lo = split(block)
            ah[ri, rj], al[ri, rj] = hi, lo
            if j > i:
                ah[rj, ri], al[rj, ri] = hi.T, lo.T
    gather_rows(messages, x_ref)
    hi, lo = split(x_ref[...])
    xh[...] = hi
    xl[...] = lo
    polynomial((ah, al), (bh, bl))
    everything = slice(0, 8 * MSG_ROWS)
    columns = [tile(q) for q in range(NT)]
    for w in columns:
        y_ref[:, w] = product(everything, w, (xh, xl), (bh, bl))
    symmetric_product((ah, al), (bh, bl), (ch, cl))
    symmetric_product((ch, cl), (bh, bl), (ah, al))
    hi, lo = split(y_ref[...])
    xh[...] = hi
    xl[...] = lo
    for w in columns:
        x_ref[:, w] = third_coef * product(everything, w, (xh, xl), (ah, al)) + second_coef * y_ref[:, w]
    factor = inverse * out_scale
    hi, lo = split(x_ref[...] * factor)
    xh[...] = hi
    xl[...] = lo
    y_ref[...] = y_ref[...] * (first_coef * factor)


def last_kernel(half, y_ref, wh, wl, gh, gl, *outs):
    start = half * 4 * MSG_ROWS
    r = slice(start, start + 4 * MSG_ROWS)
    for q in range(NT):
        result = product(r, tile(q), (wh, wl), (gh, gl)) + y_ref[r, tile(q)]
        for i, out_ref in enumerate(outs):
            for j in range(TILE // BLK):
                out_ref[pl.ds(q * (TILE // BLK) + j, MSG_ROWS, stride=NB), :] = result[
                    i * MSG_ROWS : (i + 1) * MSG_ROWS, j * BLK : (j + 1) * BLK
                ]


def update_kernel(half, table_ref, chosen_ref, i0, i1, i2, i3, *refs):
    update_ref, zero_ref, sems = refs[-3:]
    lines = pl.ds(half * LINES, LINES)
    zero_ref[...] = jnp.zeros((LINES, BLK), f32)

    def piece_copy(slot):
        source = (i0, i1, i2, i3)[slot // 4].at[pl.ds(slot % 4 * LINES, LINES)]
        return pltpu.make_async_copy(source, update_ref.at[chosen_ref[slot], lines], sems.at[slot])

    def zero_copy(k):
        return pltpu.make_async_copy(zero_ref, update_ref.at[k, lines], sems.at[GROUPS + k])

    for slot in range(GROUPS):
        piece_copy(slot).start()
    for k in range(MATS):
        pl.when(table_ref[k] >= GROUPS)(lambda k=k: zero_copy(k).start())
    for slot in range(GROUPS):
        piece_copy(slot).wait()
    for k in range(MATS):
        pl.when(table_ref[k] >= GROUPS)(lambda k=k: zero_copy(k).wait())


VMEM = pl.BlockSpec(memory_space=pltpu.VMEM)
SMEM = pl.BlockSpec(memory_space=pltpu.SMEM)
HBM = pl.BlockSpec(memory_space=pltpu.HBM)


def shape(*dims):
    return jax.ShapeDtypeStruct(dims, f32)


def call(kernel, in_specs, out_shape, scratch, name, flops, moved, mib, out_specs=None, aliases={}):
    return pl.pallas_call(
        kernel,
        in_specs=in_specs,
        out_specs=out_specs or jax.tree.map(lambda _: VMEM, out_shape),
        input_output_aliases=aliases,
        out_shape=out_shape,
        scratch_shapes=scratch,
        name=name,
        cost_estimate=pl.CostEstimate(flops=flops, bytes_accessed=moved, transcendentals=0),
        compiler_params=pltpu.CompilerParams(vmem_limit_bytes=mib * 1024 * 1024),
    )


MESSAGES = [shape(MSG_LINES, BLK)] * 4
MSG_BYTES = 8 * MSG_LINES * BLK * 4


def send_rows(messages, regroup, half):
    first, second = (second_axis, first_axis) if half else (first_axis, second_axis)
    middle = [messages[0]] + [permute(messages[s], first(s)) for s in (1, 2, 3)]
    middle = regroup(*middle)
    return [middle[0]] + [permute(middle[t], second(t)) for t in (1, 2, 3)]


def return_rows(messages, regroup, half):
    if half:
        messages = regroup(*messages)
    middle = [messages[0]] + [permute(messages[t], second_axis(-t)) for t in (1, 2, 3)]
    middle = regroup(*middle)
    return [middle[0]] + [permute(middle[s], first_axis(-s)) for s in (1, 2, 3)]


def shards(grads, momentum, owner_table):
    grp, row = lax.axis_index("grp"), lax.axis_index("row")
    core = row % 2
    place = jnp.stack([(row // 2) % 4, grp % 4, (grp // 4) * 2 + row // 8, core]).astype(jnp.int32)
    lines = (MATS, 2 * LINES, BLK)
    grads, momentum = grads.reshape(lines), momentum.reshape(lines)

    buffers = [pltpu.VMEM((MATS, LINES, BLK), f32)] * 2 + [pltpu.SemaphoreType.DMA((2,))]
    chosen, *first_rows = call(
        functools.partial(outgoing_kernel, 0), [SMEM, SMEM, HBM, HBM],
        [jax.ShapeDtypeStruct((GROUPS,), jnp.int32)] + MESSAGES, buffers,
        "outgoing", 0, 2 * MSG_BYTES, 53, [SMEM] + [VMEM] * 4,
    )(owner_table, place, grads, momentum)
    last_rows = call(
        functools.partial(outgoing_kernel, 1), [SMEM, SMEM, HBM, HBM, SMEM], MESSAGES, buffers,
        "outgoing", 0, 2 * MSG_BYTES, 51,
    )(owner_table, place, grads, momentum, chosen)

    regroup = call(regroup_kernel, [VMEM] * 4, MESSAGES, [], "regroup", 0, MSG_BYTES, 4)
    owned = send_rows(first_rows, regroup, 0) + send_rows(last_rows, regroup, 1)

    tall = [pltpu.VMEM((8 * MSG_ROWS, C), bf16)] * 2
    whole = pltpu.VMEM((8 * MSG_ROWS, C), f32)
    triangle = pltpu.VMEM((TRI * BLK, BLK), f32)
    sums = call(
        gram_kernel, [SMEM] + [VMEM] * 8, [shape(PART, BLK)] * 8,
        [whole] + tall + [pltpu.VMEM((C, 8 * MSG_ROWS), bf16)] * 2 + [triangle],
        "gram", 3 * 8 * MSG_ROWS * C * C, MSG_BYTES + 8 * PART * BLK * 4, 20,
    )(place, *owned)
    keeps, gives = sums[:4], sums[4:]

    distant = keeps[2] + swap_cores(gives[2])
    ends = keeps[3] + swap_cores(gives[3])
    distant, ends, late_near, late_middle = lax.optimization_barrier((distant, ends, gives[0], gives[1]))
    near = keeps[0] + swap_cores(late_near)
    middle = keeps[1] + swap_cores(late_middle)
    moved = [middle[:HALF] + along_z(ends[:HALF], 2) + along_z(distant[:HALF], 1)]
    moved.append(middle[HALF:] + along_z(distant[HALF:], 1))
    moved = [along_z(moved[h], 2) + along_z(near[h * HALF : (h + 1) * HALF], 1) for h in range(2)]
    moved[0] = moved[0] + ends[HALF:]
    own = [moved[0] + swap_cores(moved[1]), moved[1] + swap_cores(moved[0])]

    second = [along_z(half, 2) for half in own]
    first = [along_z(half, 1) for half in own]

    late_table, _ = lax.optimization_barrier((owner_table, own[0]))
    new_momentum = call(
        momentum_kernel, [SMEM, VMEM, VMEM], shape(*lines), [], "momentum", 0, 6 * MSG_BYTES, 12,
    )(late_table, grads, momentum)
    new_momentum, second[1] = lax.optimization_barrier((new_momentum, second[1]))

    third = [along_z(half, 1) for half in second]
    fourth = along_z(second[0], 2)
    gathered = [first[0], second[0], third[0], fourth, first[1], second[1], third[1]]
    halves = own + gathered + [swap_cores(half) for half in gathered]

    narrow = jax.ShapeDtypeStruct((8 * MSG_ROWS, C), bf16)
    square = jax.ShapeDtypeStruct((C, C), bf16)
    chained = call(
        step_kernel, [SMEM] + [VMEM] * 24, [shape(8 * MSG_ROWS, C), narrow, narrow, square, square],
        [triangle, whole] + [pltpu.VMEM((C, C), bf16)] * 4,
        "newton", 6 * (3 * C * C * C * 5 // 8 + 2 * 8 * MSG_ROWS * C * C), 2 * MSG_BYTES + 4 * TRI * BLK * BLK, 36,
    )(place, *halves, *owned)

    update = []
    for half in range(2):
        results = call(
            functools.partial(last_kernel, half), [VMEM] * 5, MESSAGES, [],
            "last", 3 * 8 * MSG_ROWS * C * C, 2 * MSG_BYTES, 12,
        )(*chained)
        back = return_rows(results, regroup, half)
        update = [
            call(
                functools.partial(update_kernel, half), [SMEM, SMEM] + [VMEM] * 4 + [HBM] * half, shape(*lines),
                [pltpu.VMEM((LINES, BLK), f32), pltpu.SemaphoreType.DMA((GROUPS + MATS,))],
                "update", 0, MSG_BYTES, 4, HBM, {6: 0} if half else {},
            )(owner_table, chosen, *back, *update)
        ]
    update = update[0]
    state = (MATS, 1, 2 * LINES * BLK // C, C)
    return (new_momentum.reshape(state), update.reshape(state))


def solution(mesh):
    in_specs = (P(None, "row", "grp", None), P(None, "row", "grp", None), P())
    out_specs = (P(None, "row", "grp", None), P(None, "row", "grp", None))
    return jax.shard_map(shards, mesh=mesh, in_specs=in_specs, out_specs=out_specs, check_vma=False)
```

```python
import functools
import math

import jax
import jax.numpy as jnp
from jax import lax
from jax.experimental import pallas as pl
from jax.experimental.pallas import tpu as pltpu
from jax.sharding import PartitionSpec as P

MATS = 24
GROUPS = 16
C = 1024
PIECE_ROWS = 14
LINES = PIECE_ROWS * C // 128
MSG_ROWS = 4 * PIECE_ROWS
MSG_LINES = 4 * LINES
BAND = 2 * MSG_ROWS
ROWS = 7168
TILE = 256
NT = C // TILE
BLK = 128
NB = C // BLK
TRI = NB * (NB + 1) // 2
PART = TRI * BLK // 8
HALF = PART // 2

momentum_decay = 0.95
norm_epsilon = 1e-07
first_coef = 3.4445
second_coef = -4.775
third_coef = 2.0315
out_scale = 0.2 * math.sqrt(max(ROWS, C))

f32 = jnp.float32
bf16 = jnp.bfloat16
ALL = ("grp", "row")


def coords(n):
    core = n % 2
    x = (n // 2) % 4
    z_lo = (n // 8) % 2
    y = (n // 16) % 4
    z_hi = n // 64
    return (x, y, z_hi * 2 + z_lo, core)


def number(x, y, z, core):
    return ((((z // 2) * 4 + y) * 2 + z % 2) * 4 + x) * 2 + core


def pairs(move):
    out = []
    for n in range(256):
        x, y, z, core = coords(n)
        out.append((n, number(*move(x, y, z, core))))
    return out


def first_axis(step):
    return pairs(
        lambda x, y, z, c: ((x + step) % 4, y, z, c) if c == 0 else (x, (y + step) % 4, z, c)
    )


def second_axis(step):
    return pairs(
        lambda x, y, z, c: (x, (y + step) % 4, z, c) if c == 0 else ((x + step) % 4, y, z, c)
    )


def permute(value, perm):
    return lax.ppermute(value, ALL, perm)


def swap_cores(value):
    return permute(value, pairs(lambda x, y, z, c: (x, y, z, 1 - c)))


def along_z(value, step):
    return permute(value, pairs(lambda x, y, z, c: (x, y, (z + step * (1 - 2 * c)) % 8, c)))


def fill_chosen(table_ref, place_ref, chosen_ref):
    x, y, core = place_ref[0], place_ref[1], place_ref[3]
    for k in range(MATS):
        owner = table_ref[k]

        @pl.when(owner < GROUPS)
        def _():
            dx = ((owner & 3) - x) & 3
            dy = ((owner >> 2) - y) & 3
            slot = jnp.where(core == 0, dx * 4 + dy, dy * 4 + dx)
            chosen_ref[slot] = k


def half_slot(half, slot):
    return slot % 4 * 4 + slot // 4 if half else slot


def outgoing_kernel(half, table_ref, place_ref, grads_ref, mom_ref, chosen_ref, o0, o1, o2, o3, gbuf, mbuf, sems):
    lines = pl.ds(half * LINES, LINES)
    grads_copy = pltpu.make_async_copy(grads_ref.at[:, lines], gbuf, sems.at[0])
    mom_copy = pltpu.make_async_copy(mom_ref.at[:, lines], mbuf, sems.at[1])
    grads_copy.start()
    mom_copy.start()
    if half == 0:
        fill_chosen(table_ref, place_ref, chosen_ref)
    grads_copy.wait()
    mom_copy.wait()
    outs = (o0, o1, o2, o3)
    for slot in range(GROUPS):
        k = chosen_ref[half_slot(half, slot)]
        g = gbuf[k]
        new = momentum_decay * mbuf[k] + g
        t = slot % 4
        outs[slot // 4][t * LINES : (t + 1) * LINES, :] = g + momentum_decay * new


def momentum_kernel(table_ref, grads_ref, mom_ref, new_ref):
    for k in range(MATS):
        m = mom_ref[k]
        new_ref[k] = jnp.where(table_ref[k] < GROUPS, momentum_decay * m + grads_ref[k], m)


def regroup_kernel(i0, i1, i2, i3, o0, o1, o2, o3):
    ins, outs = (i0, i1, i2, i3), (o0, o1, o2, o3)
    for t in range(4):
        for s in range(4):
            outs[t][s * LINES : (s + 1) * LINES, :] = ins[s][t * LINES : (t + 1) * LINES, :]


def gather_rows(messages, x_ref):
    for i, message in enumerate(messages):
        for j in range(NB):
            x_ref[i * MSG_ROWS : (i + 1) * MSG_ROWS, j * BLK : (j + 1) * BLK] = message[pl.ds(j, MSG_ROWS, stride=NB), :]


def split(value):
    hi = value.astype(bf16)
    return hi, (value - hi.astype(f32)).astype(bf16)


def dot(left, right):
    return jnp.dot(left, right, preferred_element_type=f32)


def block_index(i, j):
    return i * NB - i * (i - 1) // 2 + (j - i)


def rows(start, size):
    return pl.ds(pl.multiple_of(start, 8), size)


def gram_of(messages, start_ref, gram_ref, hi_ref, lo_ref, x_ref, hit_ref, lot_ref):
    gather_rows(messages, x_ref)
    hi, lo = split(x_ref[...])
    hi_ref[...] = hi
    lo_ref[...] = lo
    hit_ref[...] = hi_ref[...].T
    lot_ref[...] = lo_ref[...].T
    for p in range(NT):
        r = slice(p * TILE, (p + 1) * TILE)
        w = slice(p * TILE, C)
        acc = dot(hit_ref[r, :], hi_ref[:, w])
        acc = acc + dot(hit_ref[r, :], lo_ref[:, w])
        acc = acc + dot(lot_ref[r, :], hi_ref[:, w])
        for i in (2 * p, 2 * p + 1):
            for j in range(i, NB):
                b = block_index(i, j)
                block = acc[(i - 2 * p) * BLK : (i - 2 * p + 1) * BLK, (j - 2 * p) * BLK : (j - 2 * p + 1) * BLK]
                at = slice(b * BLK, (b + 1) * BLK)
                gram_ref[at, :] = block if start_ref is None else block + start_ref[at, :]


def first_gram_kernel(m0, m1, m2, m3, gram_ref, hi_ref, lo_ref, x_ref, hit_ref, lot_ref):
    gram_of((m0, m1, m2, m3), None, gram_ref, hi_ref, lo_ref, x_ref, hit_ref, lot_ref)


def second_gram_kernel(place_ref, start_ref, *refs):
    messages, keeps, gives = refs[:4], refs[4:8], refs[8:12]
    hi_ref, lo_ref, x_ref, hit_ref, lot_ref, gram_ref = refs[12:]
    gram_of(messages, start_ref, gram_ref, hi_ref, lo_ref, x_ref, hit_ref, lot_ref)
    z, core = place_ref[2], place_ref[3]
    for outs, c in ((keeps, core), (gives, 1 - core)):
        way = 1 - 2 * c
        for i in (1, 2, 3):
            d = (z + way * i) & 7
            outs[i - 1][:HALF, :] = gram_ref[rows(d * PART + c * HALF, HALF), :]
            outs[i - 1][HALF:, :] = gram_ref[rows(d * PART + (1 - c) * HALF, HALF), :]
        d = (z + 4) & 7
        outs[3][:HALF, :] = gram_ref[rows(d * PART + c * HALF, HALF), :]
        outs[3][HALF:, :] = gram_ref[rows(z * PART + c * HALF, HALF), :]


def diagonal(width):
    row = lax.broadcasted_iota(jnp.int32, (TILE, width), 0)
    col = lax.broadcasted_iota(jnp.int32, (TILE, width), 1)
    return row == col


def tile(p):
    return slice(p * TILE, (p + 1) * TILE)


def put(p, value, out):
    hi, lo = split(value)
    out[0][tile(p), p * TILE :] = hi
    out[1][tile(p), p * TILE :] = lo
    for q in range(p + 1, NT):
        out[0][tile(q), tile(p)] = hi[:, tile(q - p)].T
        out[1][tile(q), tile(p)] = lo[:, tile(q - p)].T


def product(r, w, left, right):
    acc = dot(left[0][r, :], right[0][:, w])
    acc = acc + dot(left[0][r, :], right[1][:, w])
    return acc + dot(left[1][r, :], right[0][:, w])


def polynomial(s, out):
    for p in range(NT):
        r, w = tile(p), slice(p * TILE, C)
        acc = third_coef * product(r, w, s, s)
        acc = acc + second_coef * (s[0][r, w].astype(f32) + s[1][r, w].astype(f32))
        put(p, acc + jnp.where(diagonal(C - p * TILE), first_coef, 0.0), out)


def symmetric_product(left, right, out):
    for p in range(NT):
        put(p, product(tile(p), slice(p * TILE, C), left, right), out)


def step_kernel(place_ref, *refs):
    halves, narrow = refs[:16], refs[16:20]
    y_ref, xh, xl, ah, al, gram_ref, x_ref, bh, bl, ch, cl = refs[20:]
    z, core = place_ref[2], place_ref[3]
    gram_ref[rows(z * PART + core * HALF, HALF), :] = halves[0][...]
    gram_ref[rows(z * PART + (1 - core) * HALF, HALF), :] = halves[1][...]
    for c, parts in ((core, halves[2:9]), (1 - core, halves[9:])):
        way = 1 - 2 * c
        for i, part in enumerate(parts):
            distance, half = (i + 1, c) if i < 4 else (i - 3, 1 - c)
            d = (z - way * distance) & 7
            gram_ref[rows(d * PART + half * HALF, HALF), :] = part[...]
    row = lax.broadcasted_iota(jnp.int32, (BLK, BLK), 0)
    col = lax.broadcasted_iota(jnp.int32, (BLK, BLK), 1)
    diag = jnp.zeros((BLK, BLK), f32)
    for i in range(NB):
        b = block_index(i, i)
        diag = diag + gram_ref[b * BLK : (b + 1) * BLK, :]
    diag = jnp.where(row == col, diag, 0.0)
    total = jnp.sum(jnp.sum(diag, axis=0, keepdims=True), axis=1, keepdims=True)
    inverse = 1.0 / (jnp.sqrt(total) + norm_epsilon)
    for i in range(NB):
        for j in range(i, NB):
            b = block_index(i, j)
            block = gram_ref[b * BLK : (b + 1) * BLK, :] * inverse * inverse
            ri = slice(i * BLK, (i + 1) * BLK)
            rj = slice(j * BLK, (j + 1) * BLK)
            hi, lo = split(block)
            ah[ri, rj], al[ri, rj] = hi, lo
            if j > i:
                ah[rj, ri], al[rj, ri] = hi.T, lo.T
    for h in range(2):
        at = slice(h * 4 * MSG_ROWS, (h + 1) * 4 * MSG_ROWS)
        xh[at, :] = narrow[2 * h][...]
        xl[at, :] = narrow[2 * h + 1][...]
    polynomial((ah, al), (bh, bl))
    everything = slice(0, 8 * MSG_ROWS)
    columns = [tile(q) for q in range(NT)]
    for w in columns:
        y_ref[:, w] = product(everything, w, (xh, xl), (bh, bl))
    symmetric_product((ah, al), (bh, bl), (ch, cl))
    symmetric_product((ch, cl), (bh, bl), (ah, al))
    hi, lo = split(y_ref[...])
    xh[...] = hi
    xl[...] = lo
    for w in columns:
        x_ref[:, w] = third_coef * product(everything, w, (xh, xl), (ah, al)) + second_coef * y_ref[:, w]
    factor = inverse * out_scale
    hi, lo = split(x_ref[...] * factor)
    xh[...] = hi
    xl[...] = lo
    y_ref[...] = y_ref[...] * (first_coef * factor)


def last_kernel(half, y_ref, wh, wl, gh, gl, *outs):
    start = half * 4 * MSG_ROWS
    r = slice(start, start + 4 * MSG_ROWS)
    for q in range(NT):
        result = product(r, tile(q), (wh, wl), (gh, gl)) + y_ref[r, tile(q)]
        for i, out_ref in enumerate(outs):
            for j in range(TILE // BLK):
                out_ref[pl.ds(q * (TILE // BLK) + j, MSG_ROWS, stride=NB), :] = result[
                    i * MSG_ROWS : (i + 1) * MSG_ROWS, j * BLK : (j + 1) * BLK
                ]


def update_kernel(half, table_ref, chosen_ref, i0, i1, i2, i3, *refs):
    update_ref, zero_ref, sems = refs[-3:]
    lines = pl.ds(half * LINES, LINES)
    zero_ref[...] = jnp.zeros((LINES, BLK), f32)

    def piece_copy(slot):
        source = (i0, i1, i2, i3)[slot // 4].at[pl.ds(slot % 4 * LINES, LINES)]
        return pltpu.make_async_copy(source, update_ref.at[chosen_ref[slot], lines], sems.at[slot])

    def zero_copy(k):
        return pltpu.make_async_copy(zero_ref, update_ref.at[k, lines], sems.at[GROUPS + k])

    for slot in range(GROUPS):
        piece_copy(slot).start()
    for k in range(MATS):
        pl.when(table_ref[k] >= GROUPS)(lambda k=k: zero_copy(k).start())
    for slot in range(GROUPS):
        piece_copy(slot).wait()
    for k in range(MATS):
        pl.when(table_ref[k] >= GROUPS)(lambda k=k: zero_copy(k).wait())


VMEM = pl.BlockSpec(memory_space=pltpu.VMEM)
SMEM = pl.BlockSpec(memory_space=pltpu.SMEM)
HBM = pl.BlockSpec(memory_space=pltpu.HBM)


def shape(*dims):
    return jax.ShapeDtypeStruct(dims, f32)


def call(kernel, in_specs, out_shape, scratch, name, flops, moved, mib, out_specs=None, aliases={}):
    return pl.pallas_call(
        kernel,
        in_specs=in_specs,
        out_specs=out_specs or jax.tree.map(lambda _: VMEM, out_shape),
        input_output_aliases=aliases,
        out_shape=out_shape,
        scratch_shapes=scratch,
        name=name,
        cost_estimate=pl.CostEstimate(flops=flops, bytes_accessed=moved, transcendentals=0),
        compiler_params=pltpu.CompilerParams(vmem_limit_bytes=mib * 1024 * 1024),
    )


MESSAGES = [shape(MSG_LINES, BLK)] * 4
MSG_BYTES = 8 * MSG_LINES * BLK * 4


def send_rows(messages, regroup, half):
    first, second = (second_axis, first_axis) if half else (first_axis, second_axis)
    middle = [messages[0]] + [permute(messages[s], first(s)) for s in (1, 2, 3)]
    middle = regroup(*middle)
    return [middle[0]] + [permute(middle[t], second(t)) for t in (1, 2, 3)]


def return_rows(messages, regroup, half):
    if half:
        messages = regroup(*messages)
    middle = [messages[0]] + [permute(messages[t], second_axis(-t)) for t in (1, 2, 3)]
    middle = regroup(*middle)
    return [middle[0]] + [permute(middle[s], first_axis(-s)) for s in (1, 2, 3)]


def shards(grads, momentum, owner_table):
    grp, row = lax.axis_index("grp"), lax.axis_index("row")
    core = row % 2
    place = jnp.stack([(row // 2) % 4, grp % 4, (grp // 4) * 2 + row // 8, core]).astype(jnp.int32)
    lines = (MATS, 2 * LINES, BLK)
    grads, momentum = grads.reshape(lines), momentum.reshape(lines)

    buffers = [pltpu.VMEM((MATS, LINES, BLK), f32)] * 2 + [pltpu.SemaphoreType.DMA((2,))]
    chosen, *first_rows = call(
        functools.partial(outgoing_kernel, 0), [SMEM, SMEM, HBM, HBM],
        [jax.ShapeDtypeStruct((GROUPS,), jnp.int32)] + MESSAGES, buffers,
        "outgoing", 0, 2 * MSG_BYTES, 53, [SMEM] + [VMEM] * 4,
    )(owner_table, place, grads, momentum)
    last_rows = call(
        functools.partial(outgoing_kernel, 1), [SMEM, SMEM, HBM, HBM, SMEM], MESSAGES, buffers,
        "outgoing", 0, 2 * MSG_BYTES, 51,
    )(owner_table, place, grads, momentum, chosen)

    regroup = call(regroup_kernel, [VMEM] * 4, MESSAGES, [], "regroup", 0, MSG_BYTES, 4)
    owned = [send_rows(first_rows, regroup, 0), send_rows(last_rows, regroup, 1)]

    whole = pltpu.VMEM((8 * MSG_ROWS, C), f32)
    triangle = pltpu.VMEM((TRI * BLK, BLK), f32)
    narrow = [jax.ShapeDtypeStruct((4 * MSG_ROWS, C), bf16)] * 2
    gram_scratch = [pltpu.VMEM((4 * MSG_ROWS, C), f32)] + [pltpu.VMEM((C, 4 * MSG_ROWS), bf16)] * 2
    start, *first_narrow = call(
        first_gram_kernel, [VMEM] * 4, [shape(TRI * BLK, BLK)] + narrow, gram_scratch,
        "first_gram", 3 * 4 * MSG_ROWS * C * C, MSG_BYTES, 16,
    )(*owned[0])
    *sums, last_hi, last_lo = call(
        second_gram_kernel, [SMEM] + [VMEM] * 5, [shape(PART, BLK)] * 8 + narrow, gram_scratch + [triangle],
        "second_gram", 3 * 4 * MSG_ROWS * C * C, MSG_BYTES + 8 * PART * BLK * 4, 20,
    )(place, start, *owned[1])
    keeps, gives = sums[:4], sums[4:]

    distant = keeps[2] + swap_cores(gives[2])
    ends = keeps[3] + swap_cores(gives[3])
    distant, ends, late_near, late_middle = lax.optimization_barrier((distant, ends, gives[0], gives[1]))
    near = keeps[0] + swap_cores(late_near)
    middle = keeps[1] + swap_cores(late_middle)
    moved = [middle[:HALF] + along_z(ends[:HALF], 2) + along_z(distant[:HALF], 1)]
    moved.append(middle[HALF:] + along_z(distant[HALF:], 1))
    moved = [along_z(moved[h], 2) + along_z(near[h * HALF : (h + 1) * HALF], 1) for h in range(2)]
    moved[0] = moved[0] + ends[HALF:]
    own = [moved[0] + swap_cores(moved[1]), moved[1] + swap_cores(moved[0])]

    second = [along_z(half, 2) for half in own]
    first = [along_z(half, 1) for half in own]

    late_table, _ = lax.optimization_barrier((owner_table, own[0]))
    new_momentum = call(
        momentum_kernel, [SMEM, VMEM, VMEM], shape(*lines), [], "momentum", 0, 6 * MSG_BYTES, 12,
    )(late_table, grads, momentum)
    new_momentum, second[1] = lax.optimization_barrier((new_momentum, second[1]))

    third = [along_z(half, 1) for half in second]
    fourth = along_z(second[0], 2)
    gathered = [first[0], second[0], third[0], fourth, first[1], second[1], third[1]]
    halves = own + gathered + [swap_cores(half) for half in gathered]

    tall = jax.ShapeDtypeStruct((8 * MSG_ROWS, C), bf16)
    square = jax.ShapeDtypeStruct((C, C), bf16)
    chained = call(
        step_kernel, [SMEM] + [VMEM] * 20, [shape(8 * MSG_ROWS, C), tall, tall, square, square],
        [triangle, whole] + [pltpu.VMEM((C, C), bf16)] * 4,
        "newton", 6 * (3 * C * C * C * 5 // 8 + 2 * 8 * MSG_ROWS * C * C), 2 * MSG_BYTES + 4 * TRI * BLK * BLK, 36,
    )(place, *halves, *first_narrow, last_hi, last_lo)

    update = []
    for half in range(2):
        results = call(
            functools.partial(last_kernel, half), [VMEM] * 5, MESSAGES, [],
            "last", 3 * 8 * MSG_ROWS * C * C, 2 * MSG_BYTES, 12,
        )(*chained)
        back = return_rows(results, regroup, half)
        update = [
            call(
                functools.partial(update_kernel, half), [SMEM, SMEM] + [VMEM] * 4 + [HBM] * half, shape(*lines),
                [pltpu.VMEM((LINES, BLK), f32), pltpu.SemaphoreType.DMA((GROUPS + MATS,))],
                "update", 0, MSG_BYTES, 4, HBM, {6: 0} if half else {},
            )(owner_table, chosen, *back, *update)
        ]
    update = update[0]
    state = (MATS, 1, 2 * LINES * BLK // C, C)
    return (new_momentum.reshape(state), update.reshape(state))


def solution(mesh):
    in_specs = (P(None, "row", "grp", None), P(None, "row", "grp", None), P())
    out_specs = (P(None, "row", "grp", None), P(None, "row", "grp", None))
    return jax.shard_map(shards, mesh=mesh, in_specs=in_specs, out_specs=out_specs, check_vma=False)
```

```python
import functools
import math

import jax
import jax.numpy as jnp
from jax import lax
from jax.experimental import pallas as pl
from jax.experimental.pallas import tpu as pltpu
from jax.sharding import PartitionSpec as P

MATS = 24
GROUPS = 16
C = 1024
PIECE_ROWS = 14
LINES = PIECE_ROWS * C // 128
MSG_ROWS = 4 * PIECE_ROWS
MSG_LINES = 4 * LINES
BAND = 2 * MSG_ROWS
ROWS = 7168
TILE = 256
NT = C // TILE
BLK = 128
NB = C // BLK
TRI = NB * (NB + 1) // 2
PART = TRI * BLK // 8
HALF = PART // 2

momentum_decay = 0.95
norm_epsilon = 1e-07
first_coef = 3.4445
second_coef = -4.775
third_coef = 2.0315
out_scale = 0.2 * math.sqrt(max(ROWS, C))

f32 = jnp.float32
bf16 = jnp.bfloat16
ALL = ("grp", "row")


def coords(n):
    core = n % 2
    x = (n // 2) % 4
    z_lo = (n // 8) % 2
    y = (n // 16) % 4
    z_hi = n // 64
    return (x, y, z_hi * 2 + z_lo, core)


def number(x, y, z, core):
    return ((((z // 2) * 4 + y) * 2 + z % 2) * 4 + x) * 2 + core


def pairs(move):
    out = []
    for n in range(256):
        x, y, z, core = coords(n)
        out.append((n, number(*move(x, y, z, core))))
    return out


def first_axis(step):
    return pairs(
        lambda x, y, z, c: ((x + step) % 4, y, z, c) if c == 0 else (x, (y + step) % 4, z, c)
    )


def second_axis(step):
    return pairs(
        lambda x, y, z, c: (x, (y + step) % 4, z, c) if c == 0 else ((x + step) % 4, y, z, c)
    )


def permute(value, perm):
    return lax.ppermute(value, ALL, perm)


def swap_cores(value):
    return permute(value, pairs(lambda x, y, z, c: (x, y, z, 1 - c)))


def along_z(value, step):
    return permute(value, pairs(lambda x, y, z, c: (x, y, (z + step * (1 - 2 * c)) % 8, c)))


def fill_chosen(table_ref, place_ref, chosen_ref):
    x, y, core = place_ref[0], place_ref[1], place_ref[3]
    for k in range(MATS):
        owner = table_ref[k]

        @pl.when(owner < GROUPS)
        def _():
            dx = ((owner & 3) - x) & 3
            dy = ((owner >> 2) - y) & 3
            slot = jnp.where(core == 0, dx * 4 + dy, dy * 4 + dx)
            chosen_ref[slot] = k


def half_slot(half, slot):
    return slot % 4 * 4 + slot // 4 if half else slot


def outgoing_kernel(half, table_ref, place_ref, grads_ref, mom_ref, chosen_ref, o0, o1, o2, o3, gbuf, mbuf, sems):
    lines = pl.ds(half * LINES, LINES)
    grads_copy = pltpu.make_async_copy(grads_ref.at[:, lines], gbuf, sems.at[0])
    mom_copy = pltpu.make_async_copy(mom_ref.at[:, lines], mbuf, sems.at[1])
    grads_copy.start()
    mom_copy.start()
    if half == 0:
        fill_chosen(table_ref, place_ref, chosen_ref)
    grads_copy.wait()
    mom_copy.wait()
    outs = (o0, o1, o2, o3)
    for slot in range(GROUPS):
        k = chosen_ref[half_slot(half, slot)]
        g = gbuf[k]
        new = momentum_decay * mbuf[k] + g
        t = slot % 4
        outs[slot // 4][t * LINES : (t + 1) * LINES, :] = g + momentum_decay * new


def momentum_kernel(table_ref, grads_ref, mom_ref, new_ref):
    for k in range(MATS):
        m = mom_ref[k]
        new_ref[k] = jnp.where(table_ref[k] < GROUPS, momentum_decay * m + grads_ref[k], m)


def regroup_kernel(i0, i1, i2, i3, o0, o1, o2, o3):
    ins, outs = (i0, i1, i2, i3), (o0, o1, o2, o3)
    for t in range(4):
        for s in range(4):
            outs[t][s * LINES : (s + 1) * LINES, :] = ins[s][t * LINES : (t + 1) * LINES, :]


def gather_rows(messages, x_ref):
    for i, message in enumerate(messages):
        for j in range(NB):
            x_ref[i * MSG_ROWS : (i + 1) * MSG_ROWS, j * BLK : (j + 1) * BLK] = message[pl.ds(j, MSG_ROWS, stride=NB), :]


def split(value):
    hi = value.astype(bf16)
    return hi, (value - hi.astype(f32)).astype(bf16)


def dot(left, right):
    return jnp.dot(left, right, preferred_element_type=f32)


def block_index(i, j):
    return i * NB - i * (i - 1) // 2 + (j - i)


def rows(start, size):
    return pl.ds(pl.multiple_of(start, 8), size)


def gram_of(messages, start_ref, gram_ref, hi_ref, lo_ref, x_ref, hit_ref, lot_ref):
    gather_rows(messages, x_ref)
    hi, lo = split(x_ref[...])
    hi_ref[...] = hi
    lo_ref[...] = lo
    hit_ref[...] = hi_ref[...].T
    lot_ref[...] = lo_ref[...].T
    for p in range(NT):
        r = slice(p * TILE, (p + 1) * TILE)
        w = slice(p * TILE, C)
        acc = dot(hit_ref[r, :], hi_ref[:, w])
        acc = acc + dot(hit_ref[r, :], lo_ref[:, w])
        acc = acc + dot(lot_ref[r, :], hi_ref[:, w])
        for i in (2 * p, 2 * p + 1):
            for j in range(i, NB):
                b = block_index(i, j)
                block = acc[(i - 2 * p) * BLK : (i - 2 * p + 1) * BLK, (j - 2 * p) * BLK : (j - 2 * p + 1) * BLK]
                at = slice(b * BLK, (b + 1) * BLK)
                gram_ref[at, :] = block if start_ref is None else block + start_ref[at, :]


def first_gram_kernel(m0, m1, m2, m3, gram_ref, hi_ref, lo_ref, x_ref, hit_ref, lot_ref):
    gram_of((m0, m1, m2, m3), None, gram_ref, hi_ref, lo_ref, x_ref, hit_ref, lot_ref)


def second_gram_kernel(place_ref, start_ref, *refs):
    messages, keeps, gives = refs[:4], refs[4:8], refs[8:12]
    hi_ref, lo_ref, x_ref, hit_ref, lot_ref, gram_ref = refs[12:]
    gram_of(messages, start_ref, gram_ref, hi_ref, lo_ref, x_ref, hit_ref, lot_ref)
    z, core = place_ref[2], place_ref[3]
    for outs, c in ((keeps, core), (gives, 1 - core)):
        way = 1 - 2 * c
        for i in (1, 2, 3):
            d = (z + way * i) & 7
            outs[i - 1][:HALF, :] = gram_ref[rows(d * PART + c * HALF, HALF), :]
            outs[i - 1][HALF:, :] = gram_ref[rows(d * PART + (1 - c) * HALF, HALF), :]
        d = (z + 4) & 7
        outs[3][:HALF, :] = gram_ref[rows(d * PART + c * HALF, HALF), :]
        outs[3][HALF:, :] = gram_ref[rows(z * PART + c * HALF, HALF), :]


def diagonal(width):
    row = lax.broadcasted_iota(jnp.int32, (TILE, width), 0)
    col = lax.broadcasted_iota(jnp.int32, (TILE, width), 1)
    return row == col


def tile(p):
    return slice(p * TILE, (p + 1) * TILE)


def put(p, value, out):
    hi, lo = split(value)
    out[0][tile(p), p * TILE :] = hi
    out[1][tile(p), p * TILE :] = lo
    for q in range(p + 1, NT):
        out[0][tile(q), tile(p)] = hi[:, tile(q - p)].T
        out[1][tile(q), tile(p)] = lo[:, tile(q - p)].T


def product(r, w, left, right):
    acc = dot(left[0][r, :], right[0][:, w])
    acc = acc + dot(left[0][r, :], right[1][:, w])
    return acc + dot(left[1][r, :], right[0][:, w])


def polynomial(s, out):
    for p in range(NT):
        r, w = tile(p), slice(p * TILE, C)
        acc = third_coef * product(r, w, s, s)
        acc = acc + second_coef * (s[0][r, w].astype(f32) + s[1][r, w].astype(f32))
        put(p, acc + jnp.where(diagonal(C - p * TILE), first_coef, 0.0), out)


def symmetric_product(left, right, out):
    for p in range(NT):
        put(p, product(tile(p), slice(p * TILE, C), left, right), out)


def step_kernel(place_ref, *refs):
    halves, narrow, outs = refs[:16], refs[16:20], refs[20:28]
    gram_ref, x_ref, y_ref, ah, al, bh, bl, ch, cl, xh, xl = refs[28:]
    z, core = place_ref[2], place_ref[3]
    gram_ref[rows(z * PART + core * HALF, HALF), :] = halves[0][...]
    gram_ref[rows(z * PART + (1 - core) * HALF, HALF), :] = halves[1][...]
    for c, parts in ((core, halves[2:9]), (1 - core, halves[9:])):
        way = 1 - 2 * c
        for i, part in enumerate(parts):
            distance, half = (i + 1, c) if i < 4 else (i - 3, 1 - c)
            d = (z - way * distance) & 7
            gram_ref[rows(d * PART + half * HALF, HALF), :] = part[...]
    row = lax.broadcasted_iota(jnp.int32, (BLK, BLK), 0)
    col = lax.broadcasted_iota(jnp.int32, (BLK, BLK), 1)
    diag = jnp.zeros((BLK, BLK), f32)
    for i in range(NB):
        b = block_index(i, i)
        diag = diag + gram_ref[b * BLK : (b + 1) * BLK, :]
    diag = jnp.where(row == col, diag, 0.0)
    total = jnp.sum(jnp.sum(diag, axis=0, keepdims=True), axis=1, keepdims=True)
    inverse = 1.0 / (jnp.sqrt(total) + norm_epsilon)
    for i in range(NB):
        for j in range(i, NB):
            b = block_index(i, j)
            block = gram_ref[b * BLK : (b + 1) * BLK, :] * inverse * inverse
            ri = slice(i * BLK, (i + 1) * BLK)
            rj = slice(j * BLK, (j + 1) * BLK)
            hi, lo = split(block)
            ah[ri, rj], al[ri, rj] = hi, lo
            if j > i:
                ah[rj, ri], al[rj, ri] = hi.T, lo.T
    for h in range(2):
        at = slice(h * 4 * MSG_ROWS, (h + 1) * 4 * MSG_ROWS)
        xh[at, :] = narrow[2 * h][...]
        xl[at, :] = narrow[2 * h + 1][...]
    polynomial((ah, al), (bh, bl))
    everything = slice(0, 8 * MSG_ROWS)
    columns = [tile(q) for q in range(NT)]
    for w in columns:
        y_ref[:, w] = product(everything, w, (xh, xl), (bh, bl))
    symmetric_product((ah, al), (bh, bl), (ch, cl))
    symmetric_product((ch, cl), (bh, bl), (ah, al))
    hi, lo = split(y_ref[...])
    xh[...] = hi
    xl[...] = lo
    for w in columns:
        x_ref[:, w] = third_coef * product(everything, w, (xh, xl), (ah, al)) + second_coef * y_ref[:, w]
    hi, lo = split(x_ref[...])
    xh[...] = hi
    xl[...] = lo
    factor = inverse * out_scale
    for q, w in enumerate(columns):
        result = (product(everything, w, (xh, xl), (ah, al)) + first_coef * y_ref[:, w]) * factor
        for i, out_ref in enumerate(outs):
            for j in range(TILE // BLK):
                out_ref[pl.ds(q * (TILE // BLK) + j, MSG_ROWS, stride=NB), :] = result[
                    i * MSG_ROWS : (i + 1) * MSG_ROWS, j * BLK : (j + 1) * BLK
                ]


def update_kernel(half, table_ref, chosen_ref, i0, i1, i2, i3, *refs):
    update_ref, zero_ref, sems = refs[-3:]
    lines = pl.ds(half * LINES, LINES)

    def piece_copy(slot):
        source = (i0, i1, i2, i3)[slot // 4].at[pl.ds(slot % 4 * LINES, LINES)]
        return pltpu.make_async_copy(source, update_ref.at[chosen_ref[slot], lines], sems.at[slot])

    def zero_copy(k):
        return pltpu.make_async_copy(zero_ref, update_ref.at[k], sems.at[GROUPS + k])

    for slot in range(GROUPS):
        piece_copy(slot).start()
    if half == 0:
        zero_ref[...] = jnp.zeros((2 * LINES, BLK), f32)
        for k in range(MATS):
            pl.when(table_ref[k] >= GROUPS)(lambda k=k: zero_copy(k).start())
    for slot in range(GROUPS):
        piece_copy(slot).wait()
    if half == 0:
        for k in range(MATS):
            pl.when(table_ref[k] >= GROUPS)(lambda k=k: zero_copy(k).wait())


VMEM = pl.BlockSpec(memory_space=pltpu.VMEM)
SMEM = pl.BlockSpec(memory_space=pltpu.SMEM)
HBM = pl.BlockSpec(memory_space=pltpu.HBM)


def shape(*dims):
    return jax.ShapeDtypeStruct(dims, f32)


def call(kernel, in_specs, out_shape, scratch, name, flops, moved, mib, out_specs=None, aliases={}):
    return pl.pallas_call(
        kernel,
        in_specs=in_specs,
        out_specs=out_specs or jax.tree.map(lambda _: VMEM, out_shape),
        input_output_aliases=aliases,
        out_shape=out_shape,
        scratch_shapes=scratch,
        name=name,
        cost_estimate=pl.CostEstimate(flops=flops, bytes_accessed=moved, transcendentals=0),
        compiler_params=pltpu.CompilerParams(vmem_limit_bytes=mib * 1024 * 1024),
    )


MESSAGES = [shape(MSG_LINES, BLK)] * 4
MSG_BYTES = 8 * MSG_LINES * BLK * 4


def send_rows(messages, regroup, half):
    first, second = (second_axis, first_axis) if half else (first_axis, second_axis)
    middle = [messages[0]] + [permute(messages[s], first(s)) for s in (1, 2, 3)]
    middle = regroup(*middle)
    return [middle[0]] + [permute(middle[t], second(t)) for t in (1, 2, 3)]


def return_rows(messages, regroup, half):
    if half:
        messages = regroup(*messages)
    middle = [messages[0]] + [permute(messages[t], second_axis(-t)) for t in (1, 2, 3)]
    middle = regroup(*middle)
    return [middle[0]] + [permute(middle[s], first_axis(-s)) for s in (1, 2, 3)]


def shards(grads, momentum, owner_table):
    grp, row = lax.axis_index("grp"), lax.axis_index("row")
    core = row % 2
    place = jnp.stack([(row // 2) % 4, grp % 4, (grp // 4) * 2 + row // 8, core]).astype(jnp.int32)
    lines = (MATS, 2 * LINES, BLK)
    grads, momentum = grads.reshape(lines), momentum.reshape(lines)

    buffers = [pltpu.VMEM((MATS, LINES, BLK), f32)] * 2 + [pltpu.SemaphoreType.DMA((2,))]
    chosen, *first_rows = call(
        functools.partial(outgoing_kernel, 0), [SMEM, SMEM, HBM, HBM],
        [jax.ShapeDtypeStruct((GROUPS,), jnp.int32)] + MESSAGES, buffers,
        "outgoing", 0, 2 * MSG_BYTES, 53, [SMEM] + [VMEM] * 4,
    )(owner_table, place, grads, momentum)
    last_rows = call(
        functools.partial(outgoing_kernel, 1), [SMEM, SMEM, HBM, HBM, SMEM], MESSAGES, buffers,
        "outgoing", 0, 2 * MSG_BYTES, 51,
    )(owner_table, place, grads, momentum, chosen)

    regroup = call(regroup_kernel, [VMEM] * 4, MESSAGES, [], "regroup", 0, MSG_BYTES, 4)
    owned = [send_rows(first_rows, regroup, 0), send_rows(last_rows, regroup, 1)]

    whole = pltpu.VMEM((8 * MSG_ROWS, C), f32)
    triangle = pltpu.VMEM((TRI * BLK, BLK), f32)
    narrow = [jax.ShapeDtypeStruct((4 * MSG_ROWS, C), bf16)] * 2
    gram_scratch = [pltpu.VMEM((4 * MSG_ROWS, C), f32)] + [pltpu.VMEM((C, 4 * MSG_ROWS), bf16)] * 2
    start, *first_narrow = call(
        first_gram_kernel, [VMEM] * 4, [shape(TRI * BLK, BLK)] + narrow, gram_scratch,
        "first_gram", 3 * 4 * MSG_ROWS * C * C, MSG_BYTES, 16,
    )(*owned[0])
    *sums, last_hi, last_lo = call(
        second_gram_kernel, [SMEM] + [VMEM] * 5, [shape(PART, BLK)] * 8 + narrow, gram_scratch + [triangle],
        "second_gram", 3 * 4 * MSG_ROWS * C * C, MSG_BYTES + 8 * PART * BLK * 4, 20,
    )(place, start, *owned[1])
    keeps, gives = sums[:4], sums[4:]

    distant = keeps[2] + swap_cores(gives[2])
    ends = keeps[3] + swap_cores(gives[3])
    distant, ends, late_near, late_middle = lax.optimization_barrier((distant, ends, gives[0], gives[1]))
    near = keeps[0] + swap_cores(late_near)
    middle = keeps[1] + swap_cores(late_middle)
    moved = [middle[:HALF] + along_z(ends[:HALF], 2) + along_z(distant[:HALF], 1)]
    moved.append(middle[HALF:] + along_z(distant[HALF:], 1))
    moved = [along_z(moved[h], 2) + along_z(near[h * HALF : (h + 1) * HALF], 1) for h in range(2)]
    moved[0] = moved[0] + ends[HALF:]
    own = [moved[0] + swap_cores(moved[1]), moved[1] + swap_cores(moved[0])]

    second = [along_z(half, 2) for half in own]
    first = [along_z(half, 1) for half in own]

    late_table, _ = lax.optimization_barrier((owner_table, own[0]))
    new_momentum = call(
        momentum_kernel, [SMEM, VMEM, VMEM], shape(*lines), [], "momentum", 0, 6 * MSG_BYTES, 12,
    )(late_table, grads, momentum)
    new_momentum, second[1] = lax.optimization_barrier((new_momentum, second[1]))

    third = [along_z(half, 1) for half in second]
    fourth = along_z(second[0], 2)
    gathered = [first[0], second[0], third[0], fourth, first[1], second[1], third[1]]
    halves = own + gathered + [swap_cores(half) for half in gathered]

    results = call(
        step_kernel, [SMEM] + [VMEM] * 20, MESSAGES * 2,
        [triangle, whole, whole] + [pltpu.VMEM((C, C), bf16)] * 6 + [pltpu.VMEM((8 * MSG_ROWS, C), bf16)] * 2,
        "newton", 6 * (3 * C * C * C * 5 // 8 + 3 * 8 * MSG_ROWS * C * C), 2 * MSG_BYTES + 4 * TRI * BLK * BLK, 36,
    )(place, *halves, *first_narrow, last_hi, last_lo)

    update = []
    for half in range(2):
        back = return_rows(results[4 * half : 4 * half + 4], regroup, half)
        update = [
            call(
                functools.partial(update_kernel, half), [SMEM, SMEM] + [VMEM] * 4 + [HBM] * half, shape(*lines),
                [pltpu.VMEM((2 * LINES, BLK), f32), pltpu.SemaphoreType.DMA((GROUPS + MATS,))],
                "update", 0, MSG_BYTES, 4, HBM, {6: 0} if half else {},
            )(owner_table, chosen, *back, *update)
        ]
    update = update[0]
    state = (MATS, 1, 2 * LINES * BLK // C, C)
    return (new_momentum.reshape(state), update.reshape(state))


def solution(mesh):
    in_specs = (P(None, "row", "grp", None), P(None, "row", "grp", None), P())
    out_specs = (P(None, "row", "grp", None), P(None, "row", "grp", None))
    return jax.shard_map(shards, mesh=mesh, in_specs=in_specs, out_specs=out_specs, check_vma=False)
```

```python
import functools
import math

import jax
import jax.numpy as jnp
from jax import lax
from jax.experimental import pallas as pl
from jax.experimental.pallas import tpu as pltpu
from jax.sharding import PartitionSpec as P

MATS = 24
GROUPS = 16
C = 1024
PIECE_ROWS = 14
LINES = PIECE_ROWS * C // 128
MSG_ROWS = 4 * PIECE_ROWS
MSG_LINES = 4 * LINES
BAND = 2 * MSG_ROWS
ROWS = 7168
TILE = 256
NT = C // TILE
BLK = 128
NB = C // BLK
TRI = NB * (NB + 1) // 2
PART = TRI * BLK // 8
HALF = PART // 2

momentum_decay = 0.95
norm_epsilon = 1e-07
first_coef = 3.4445
second_coef = -4.775
third_coef = 2.0315
out_scale = 0.2 * math.sqrt(max(ROWS, C))

f32 = jnp.float32
bf16 = jnp.bfloat16
ALL = ("grp", "row")


def coords(n):
    core = n % 2
    x = (n // 2) % 4
    z_lo = (n // 8) % 2
    y = (n // 16) % 4
    z_hi = n // 64
    return (x, y, z_hi * 2 + z_lo, core)


def number(x, y, z, core):
    return ((((z // 2) * 4 + y) * 2 + z % 2) * 4 + x) * 2 + core


def pairs(move):
    out = []
    for n in range(256):
        x, y, z, core = coords(n)
        out.append((n, number(*move(x, y, z, core))))
    return out


def first_axis(step):
    return pairs(
        lambda x, y, z, c: ((x + step) % 4, y, z, c) if c == 0 else (x, (y + step) % 4, z, c)
    )


def second_axis(step):
    return pairs(
        lambda x, y, z, c: (x, (y + step) % 4, z, c) if c == 0 else ((x + step) % 4, y, z, c)
    )


def permute(value, perm):
    return lax.ppermute(value, ALL, perm)


def swap_cores(value):
    return permute(value, pairs(lambda x, y, z, c: (x, y, z, 1 - c)))


def along_z(value, step):
    return permute(value, pairs(lambda x, y, z, c: (x, y, (z + step * (1 - 2 * c)) % 8, c)))


def fill_chosen(table_ref, place_ref, chosen_ref):
    x, y, core = place_ref[0], place_ref[1], place_ref[3]
    for k in range(MATS):
        owner = table_ref[k]

        @pl.when(owner < GROUPS)
        def _():
            dx = ((owner & 3) - x) & 3
            dy = ((owner >> 2) - y) & 3
            slot = jnp.where(core == 0, dx * 4 + dy, dy * 4 + dx)
            chosen_ref[slot] = k


def half_slot(half, slot):
    return slot % 4 * 4 + slot // 4 if half else slot


def outgoing_kernel(table_ref, place_ref, grads_ref, mom_ref, chosen_ref, *refs):
    outs, (gbuf, mbuf, sems) = refs[:8], refs[8:]

    def copies(half):
        lines = pl.ds(half * LINES, LINES)
        return (
            pltpu.make_async_copy(grads_ref.at[:, lines], gbuf.at[half], sems.at[0, half]),
            pltpu.make_async_copy(mom_ref.at[:, lines], mbuf.at[half], sems.at[1, half]),
        )

    for half in range(2):
        for copy in copies(half):
            copy.start()
    fill_chosen(table_ref, place_ref, chosen_ref)
    for half in range(2):
        for copy in copies(half):
            copy.wait()
        for slot in range(GROUPS):
            k = chosen_ref[half_slot(half, slot)]
            g = gbuf[half, k]
            new = momentum_decay * mbuf[half, k] + g
            t = slot % 4
            outs[4 * half + slot // 4][t * LINES : (t + 1) * LINES, :] = g + momentum_decay * new


def momentum_kernel(table_ref, grads_ref, mom_ref, new_ref):
    for k in range(MATS):
        m = mom_ref[k]
        new_ref[k] = jnp.where(table_ref[k] < GROUPS, momentum_decay * m + grads_ref[k], m)


def regroup_kernel(i0, i1, i2, i3, o0, o1, o2, o3):
    ins, outs = (i0, i1, i2, i3), (o0, o1, o2, o3)
    for t in range(4):
        for s in range(4):
            outs[t][s * LINES : (s + 1) * LINES, :] = ins[s][t * LINES : (t + 1) * LINES, :]


def gather_rows(messages, x_ref):
    for i, message in enumerate(messages):
        for j in range(NB):
            x_ref[i * MSG_ROWS : (i + 1) * MSG_ROWS, j * BLK : (j + 1) * BLK] = message[pl.ds(j, MSG_ROWS, stride=NB), :]


def split(value):
    hi = value.astype(bf16)
    return hi, (value - hi.astype(f32)).astype(bf16)


def dot(left, right):
    return jnp.dot(left, right, preferred_element_type=f32)


def block_index(i, j):
    return i * NB - i * (i - 1) // 2 + (j - i)


def rows(start, size):
    return pl.ds(pl.multiple_of(start, 8), size)


def gram_of(messages, start_ref, gram_ref, hi_ref, lo_ref, x_ref, hit_ref, lot_ref):
    gather_rows(messages, x_ref)
    hi, lo = split(x_ref[...])
    hi_ref[...] = hi
    lo_ref[...] = lo
    hit_ref[...] = hi_ref[...].T
    lot_ref[...] = lo_ref[...].T
    for p in range(NT):
        r = slice(p * TILE, (p + 1) * TILE)
        w = slice(p * TILE, C)
        acc = dot(hit_ref[r, :], hi_ref[:, w])
        acc = acc + dot(hit_ref[r, :], lo_ref[:, w])
        acc = acc + dot(lot_ref[r, :], hi_ref[:, w])
        for i in (2 * p, 2 * p + 1):
            for j in range(i, NB):
                b = block_index(i, j)
                block = acc[(i - 2 * p) * BLK : (i - 2 * p + 1) * BLK, (j - 2 * p) * BLK : (j - 2 * p + 1) * BLK]
                at = slice(b * BLK, (b + 1) * BLK)
                gram_ref[at, :] = block if start_ref is None else block + start_ref[at, :]


def first_gram_kernel(m0, m1, m2, m3, gram_ref, hi_ref, lo_ref, x_ref, hit_ref, lot_ref):
    gram_of((m0, m1, m2, m3), None, gram_ref, hi_ref, lo_ref, x_ref, hit_ref, lot_ref)


def second_gram_kernel(place_ref, start_ref, *refs):
    messages, keeps, gives = refs[:4], refs[4:8], refs[8:12]
    hi_ref, lo_ref, x_ref, hit_ref, lot_ref, gram_ref = refs[12:]
    gram_of(messages, start_ref, gram_ref, hi_ref, lo_ref, x_ref, hit_ref, lot_ref)
    z, core = place_ref[2], place_ref[3]
    for outs, c in ((keeps, core), (gives, 1 - core)):
        way = 1 - 2 * c
        for i in (1, 2, 3):
            d = (z + way * i) & 7
            outs[i - 1][:HALF, :] = gram_ref[rows(d * PART + c * HALF, HALF), :]
            outs[i - 1][HALF:, :] = gram_ref[rows(d * PART + (1 - c) * HALF, HALF), :]
        d = (z + 4) & 7
        outs[3][:HALF, :] = gram_ref[rows(d * PART + c * HALF, HALF), :]
        outs[3][HALF:, :] = gram_ref[rows(z * PART + c * HALF, HALF), :]


def diagonal(width):
    row = lax.broadcasted_iota(jnp.int32, (TILE, width), 0)
    col = lax.broadcasted_iota(jnp.int32, (TILE, width), 1)
    return row == col


def tile(p):
    return slice(p * TILE, (p + 1) * TILE)


def put(p, value, out):
    hi, lo = split(value)
    out[0][tile(p), p * TILE :] = hi
    out[1][tile(p), p * TILE :] = lo
    for q in range(p + 1, NT):
        out[0][tile(q), tile(p)] = hi[:, tile(q - p)].T
        out[1][tile(q), tile(p)] = lo[:, tile(q - p)].T


def product(r, w, left, right):
    acc = dot(left[0][r, :], right[0][:, w])
    acc = acc + dot(left[0][r, :], right[1][:, w])
    return acc + dot(left[1][r, :], right[0][:, w])


def polynomial(s, out):
    for p in range(NT):
        r, w = tile(p), slice(p * TILE, C)
        acc = third_coef * product(r, w, s, s)
        acc = acc + second_coef * (s[0][r, w].astype(f32) + s[1][r, w].astype(f32))
        put(p, acc + jnp.where(diagonal(C - p * TILE), first_coef, 0.0), out)


def symmetric_product(left, right, out):
    for p in range(NT):
        put(p, product(tile(p), slice(p * TILE, C), left, right), out)


def step_kernel(place_ref, *refs):
    halves, narrow, outs = refs[:16], refs[16:20], refs[20:28]
    gram_ref, x_ref, y_ref, ah, al, bh, bl, ch, cl, xh, xl = refs[28:]
    z, core = place_ref[2], place_ref[3]
    gram_ref[rows(z * PART + core * HALF, HALF), :] = halves[0][...]
    gram_ref[rows(z * PART + (1 - core) * HALF, HALF), :] = halves[1][...]
    for c, parts in ((core, halves[2:9]), (1 - core, halves[9:])):
        way = 1 - 2 * c
        for i, part in enumerate(parts):
            distance, half = (i + 1, c) if i < 4 else (i - 3, 1 - c)
            d = (z - way * distance) & 7
            gram_ref[rows(d * PART + half * HALF, HALF), :] = part[...]
    row = lax.broadcasted_iota(jnp.int32, (BLK, BLK), 0)
    col = lax.broadcasted_iota(jnp.int32, (BLK, BLK), 1)
    diag = jnp.zeros((BLK, BLK), f32)
    for i in range(NB):
        b = block_index(i, i)
        diag = diag + gram_ref[b * BLK : (b + 1) * BLK, :]
    diag = jnp.where(row == col, diag, 0.0)
    total = jnp.sum(jnp.sum(diag, axis=0, keepdims=True), axis=1, keepdims=True)
    inverse = 1.0 / (jnp.sqrt(total) + norm_epsilon)
    for i in range(NB):
        for j in range(i, NB):
            b = block_index(i, j)
            block = gram_ref[b * BLK : (b + 1) * BLK, :] * inverse * inverse
            ri = slice(i * BLK, (i + 1) * BLK)
            rj = slice(j * BLK, (j + 1) * BLK)
            hi, lo = split(block)
            ah[ri, rj], al[ri, rj] = hi, lo
            if j > i:
                ah[rj, ri], al[rj, ri] = hi.T, lo.T
    for h in range(2):
        at = slice(h * 4 * MSG_ROWS, (h + 1) * 4 * MSG_ROWS)
        xh[at, :] = narrow[2 * h][...]
        xl[at, :] = narrow[2 * h + 1][...]
    polynomial((ah, al), (bh, bl))
    everything = slice(0, 8 * MSG_ROWS)
    columns = [tile(q) for q in range(NT)]
    for w in columns:
        y_ref[:, w] = product(everything, w, (xh, xl), (bh, bl))
    symmetric_product((ah, al), (bh, bl), (ch, cl))
    symmetric_product((ch, cl), (bh, bl), (ah, al))
    hi, lo = split(y_ref[...])
    xh[...] = hi
    xl[...] = lo
    for w in columns:
        x_ref[:, w] = third_coef * product(everything, w, (xh, xl), (ah, al)) + second_coef * y_ref[:, w]
    hi, lo = split(x_ref[...])
    xh[...] = hi
    xl[...] = lo
    factor = inverse * out_scale
    for q, w in enumerate(columns):
        result = (product(everything, w, (xh, xl), (ah, al)) + first_coef * y_ref[:, w]) * factor
        for i, out_ref in enumerate(outs):
            for j in range(TILE // BLK):
                out_ref[pl.ds(q * (TILE // BLK) + j, MSG_ROWS, stride=NB), :] = result[
                    i * MSG_ROWS : (i + 1) * MSG_ROWS, j * BLK : (j + 1) * BLK
                ]


def update_kernel(half, table_ref, chosen_ref, i0, i1, i2, i3, *refs):
    update_ref, zero_ref, sems = refs[-3:]
    lines = pl.ds(half * LINES, LINES)

    def piece_copy(slot):
        source = (i0, i1, i2, i3)[slot // 4].at[pl.ds(slot % 4 * LINES, LINES)]
        return pltpu.make_async_copy(source, update_ref.at[chosen_ref[slot], lines], sems.at[slot])

    def zero_copy(k):
        return pltpu.make_async_copy(zero_ref, update_ref.at[k], sems.at[GROUPS + k])

    for slot in range(GROUPS):
        piece_copy(slot).start()
    if half == 0:
        zero_ref[...] = jnp.zeros((2 * LINES, BLK), f32)
        for k in range(MATS):
            pl.when(table_ref[k] >= GROUPS)(lambda k=k: zero_copy(k).start())
    for slot in range(GROUPS):
        piece_copy(slot).wait()
    if half == 0:
        for k in range(MATS):
            pl.when(table_ref[k] >= GROUPS)(lambda k=k: zero_copy(k).wait())


VMEM = pl.BlockSpec(memory_space=pltpu.VMEM)
SMEM = pl.BlockSpec(memory_space=pltpu.SMEM)
HBM = pl.BlockSpec(memory_space=pltpu.HBM)


def shape(*dims):
    return jax.ShapeDtypeStruct(dims, f32)


def call(kernel, in_specs, out_shape, scratch, name, flops, moved, mib, out_specs=None, aliases={}):
    return pl.pallas_call(
        kernel,
        in_specs=in_specs,
        out_specs=out_specs or jax.tree.map(lambda _: VMEM, out_shape),
        input_output_aliases=aliases,
        out_shape=out_shape,
        scratch_shapes=scratch,
        name=name,
        cost_estimate=pl.CostEstimate(flops=flops, bytes_accessed=moved, transcendentals=0),
        compiler_params=pltpu.CompilerParams(vmem_limit_bytes=mib * 1024 * 1024),
    )


MESSAGES = [shape(MSG_LINES, BLK)] * 4
MSG_BYTES = 8 * MSG_LINES * BLK * 4


def send_rows(messages, regroup, half):
    first, second = (second_axis, first_axis) if half else (first_axis, second_axis)
    middle = [messages[0]] + [permute(messages[s], first(s)) for s in (1, 2, 3)]
    middle = regroup(*middle)
    return [middle[0]] + [permute(middle[t], second(t)) for t in (1, 2, 3)]


def return_rows(messages, regroup, half):
    if half:
        messages = regroup(*messages)
    middle = [messages[0]] + [permute(messages[t], second_axis(-t)) for t in (1, 2, 3)]
    middle = regroup(*middle)
    return [middle[0]] + [permute(middle[s], first_axis(-s)) for s in (1, 2, 3)]


def shards(grads, momentum, owner_table):
    grp, row = lax.axis_index("grp"), lax.axis_index("row")
    core = row % 2
    place = jnp.stack([(row // 2) % 4, grp % 4, (grp // 4) * 2 + row // 8, core]).astype(jnp.int32)
    lines = (MATS, 2 * LINES, BLK)
    grads, momentum = grads.reshape(lines), momentum.reshape(lines)

    chosen, *outgoing = call(
        outgoing_kernel, [SMEM, SMEM, HBM, HBM],
        [jax.ShapeDtypeStruct((GROUPS,), jnp.int32)] + MESSAGES * 2,
        [pltpu.VMEM((2, MATS, LINES, BLK), f32)] * 2 + [pltpu.SemaphoreType.DMA((2, 2))],
        "outgoing", 0, 3 * MSG_BYTES, 52, [SMEM] + [VMEM] * 8,
    )(owner_table, place, grads, momentum)

    regroup = call(regroup_kernel, [VMEM] * 4, MESSAGES, [], "regroup", 0, MSG_BYTES, 4)
    owned = [send_rows(outgoing[:4], regroup, 0), send_rows(outgoing[4:], regroup, 1)]

    whole = pltpu.VMEM((8 * MSG_ROWS, C), f32)
    triangle = pltpu.VMEM((TRI * BLK, BLK), f32)
    narrow = [jax.ShapeDtypeStruct((4 * MSG_ROWS, C), bf16)] * 2
    gram_scratch = [pltpu.VMEM((4 * MSG_ROWS, C), f32)] + [pltpu.VMEM((C, 4 * MSG_ROWS), bf16)] * 2
    start, *first_narrow = call(
        first_gram_kernel, [VMEM] * 4, [shape(TRI * BLK, BLK)] + narrow, gram_scratch,
        "first_gram", 3 * 4 * MSG_ROWS * C * C, MSG_BYTES, 16,
    )(*owned[0])
    *sums, last_hi, last_lo = call(
        second_gram_kernel, [SMEM] + [VMEM] * 5, [shape(PART, BLK)] * 8 + narrow, gram_scratch + [triangle],
        "second_gram", 3 * 4 * MSG_ROWS * C * C, MSG_BYTES + 8 * PART * BLK * 4, 20,
    )(place, start, *owned[1])
    keeps, gives = sums[:4], sums[4:]

    distant = keeps[2] + swap_cores(gives[2])
    ends = keeps[3] + swap_cores(gives[3])
    distant, ends, late_near, late_middle = lax.optimization_barrier((distant, ends, gives[0], gives[1]))
    near = keeps[0] + swap_cores(late_near)
    middle = keeps[1] + swap_cores(late_middle)
    moved = [middle[:HALF] + along_z(ends[:HALF], 2) + along_z(distant[:HALF], 1)]
    moved.append(middle[HALF:] + along_z(distant[HALF:], 1))
    moved = [along_z(moved[h], 2) + along_z(near[h * HALF : (h + 1) * HALF], 1) for h in range(2)]
    moved[0] = moved[0] + ends[HALF:]
    own = [moved[0] + swap_cores(moved[1]), moved[1] + swap_cores(moved[0])]

    second = [along_z(half, 2) for half in own]
    first = [along_z(half, 1) for half in own]

    late_table, _ = lax.optimization_barrier((owner_table, own[0]))
    new_momentum = call(
        momentum_kernel, [SMEM, VMEM, VMEM], shape(*lines), [], "momentum", 0, 6 * MSG_BYTES, 12,
    )(late_table, grads, momentum)
    new_momentum, second[1] = lax.optimization_barrier((new_momentum, second[1]))

    third = [along_z(half, 1) for half in second]
    fourth = along_z(second[0], 2)
    gathered = [first[0], second[0], third[0], fourth, first[1], second[1], third[1]]
    halves = own + gathered + [swap_cores(half) for half in gathered]

    results = call(
        step_kernel, [SMEM] + [VMEM] * 20, MESSAGES * 2,
        [triangle, whole, whole] + [pltpu.VMEM((C, C), bf16)] * 6 + [pltpu.VMEM((8 * MSG_ROWS, C), bf16)] * 2,
        "newton", 6 * (3 * C * C * C * 5 // 8 + 3 * 8 * MSG_ROWS * C * C), 2 * MSG_BYTES + 4 * TRI * BLK * BLK, 36,
    )(place, *halves, *first_narrow, last_hi, last_lo)

    update = []
    for half in range(2):
        back = return_rows(results[4 * half : 4 * half + 4], regroup, half)
        update = [
            call(
                functools.partial(update_kernel, half), [SMEM, SMEM] + [VMEM] * 4 + [HBM] * half, shape(*lines),
                [pltpu.VMEM((2 * LINES, BLK), f32), pltpu.SemaphoreType.DMA((GROUPS + MATS,))],
                "update", 0, MSG_BYTES, 4, HBM, {6: 0} if half else {},
            )(owner_table, chosen, *back, *update)
        ]
    update = update[0]
    state = (MATS, 1, 2 * LINES * BLK // C, C)
    return (new_momentum.reshape(state), update.reshape(state))


def solution(mesh):
    in_specs = (P(None, "row", "grp", None), P(None, "row", "grp", None), P())
    out_specs = (P(None, "row", "grp", None), P(None, "row", "grp", None))
    return jax.shard_map(shards, mesh=mesh, in_specs=in_specs, out_specs=out_specs, check_vma=False)
```
